32 devices in a mesh: ctx: 16 (over z, y, x), head: 2 (over core).
Axes of the slice: x: 2, y: 2, z: 4, core: 2. Of those that a mesh axis runs over, the one named last changes fastest.
Arguments:
- query_rows: bfloat16 [8192, 512], P('ctx', 'head'), parts along dimension 1, may hold values from -6 to 6
- key_rows: bfloat16 [8192, 512], P('ctx', 'head'), parts along dimension 1, may hold values from -6 to 6
- value_rows: bfloat16 [8192, 512], P('ctx', 'head'), parts along dimension 1, may hold values from -6 to 6
- out_grad: bfloat16 [8192, 512], P('ctx', 'head'), parts along dimension 1, may hold values from -6 to 6
- doc_lengths: int32 [16], P('head'), parts along dimension 0, may hold values from 1 to 2048, 8192 in all
Outputs:
- attended: bfloat16 [8192, 512], P('ctx', 'head'), parts along dimension 1
- grad_query: bfloat16 [8192, 512], P('ctx', 'head'), parts along dimension 1
- grad_key: bfloat16 [8192, 512], P('ctx', 'head'), parts along dimension 1
- grad_value: bfloat16 [8192, 512], P('ctx', 'head'), parts along dimension 1
The draws below stay inside these ranges and needn't reach their ends.
There are 2 independent parts, one for each index of `head`. The reference program is written for one: setup_inputs(seed, part) draws one part's arguments, and reference() takes and returns one part's arrays. A program takes and returns all parts, laid end to end along the dimension named above; each array names one. Nothing has to cross between parts.
Inputs may be any that keep to these rules, and one draw needn't show every extreme that they name: `doc_lengths`: the lengths add up to 8192; the longest document holds exactly 2048 tokens.
All inputs are finite; a program needn't handle non-finite values.
Results may differ from the reference program's by a relative error of at most 0.0051.
Values sent between devices are 32-bit elements; how exact they have to be, the bound alone decides.
No kernel may reach another device: no remote copies, remote signals or barrier semaphores. Data moves between devices by JAX's collectives and lax.ppermute only.
A program may use at most 64 MiB of HBM per device.

```python
import math
import jax
import jax.numpy as jnp
import numpy as np
from jax import lax

HD = 128
HEADS = 2
TOK_DEV = 512
DOCS = 8
TOKENS = 8192
DOC_MOST = 2048
N_CTX = 16


def steps_of(rng, shape, cuts, smallest, largest):
    loudness, own = 1.0, jax.random.fold_in(rng, 6)
    for axis_at, blocks in cuts:
        draws = jnp.exp(jax.random.uniform(jax.random.fold_in(own, axis_at), (blocks,), jnp.float32, smallest / len(cuts), largest / len(cuts)))
        loudness = loudness * jnp.repeat(draws, shape[axis_at] // blocks).reshape([-1 if axis == axis_at else 1 for axis in range(len(shape))])
    return loudness


def split_up(number_of, total, bound, lean):
    portions = [(1 << 20) // math.isqrt(rank ** lean) + 1 for rank in range(2, number_of + 1)]
    spare, given = total - bound - (number_of - 1), [1] * (number_of - 1)
    while spare > 0:
        free = [i for i in range(number_of - 1) if given[i] < bound]
        mass, budget = sum([portions[i] for i in free]), spare
        for i in free:
            addition = min(bound - given[i], max(1, budget * portions[i] // mass), spare)
            given[i] = given[i] + addition
            spare = spare - addition
    return np.array([bound] + given)


def ragged(rng, count, total, bound, skew):
    if count == 2:
        one = jax.random.randint(rng, (), max(1, total - bound), min(bound, total - 1) + 1)
        return jnp.stack([one, total - one])
    lengths = jnp.asarray(split_up(count, total, bound, skew), jnp.int32)
    pairs = (count - 1) // 2
    donor, sink = lengths[1:1 + 2 * pairs:2], lengths[2:2 + 2 * pairs:2]
    room = jnp.minimum(donor - 1, bound - sink)
    shifted = jax.random.randint(jax.random.fold_in(rng, 1), (pairs,), 0, 1 << 20) % (room + 1)
    lengths = lengths.at[1:1 + 2 * pairs:2].set(donor - shifted).at[2:2 + 2 * pairs:2].set(sink + shifted)
    return lengths[jax.random.permutation(jax.random.fold_in(rng, 2), count)]


def scatter_about(own_key, extent, deviation, limit, pieces=(), kind=jnp.bfloat16):
    drawn = deviation * jax.random.normal(own_key, extent, jnp.float32)
    if pieces:
        drawn = drawn * steps_of(own_key, extent, pieces, -0.22, 0.18)
    return jnp.clip(drawn, -limit, limit).astype(kind)


def setup_inputs(seed: int = 0, part: int = 0) -> dict:
    streams_of = jax.random.split(jax.random.key(seed), 6)
    part_splits = jax.random.split(jax.random.fold_in(streams_of[5], part), 6)
    return {
        "query_rows": scatter_about(part_splits[0], (TOKENS, HEADS * HD), 1.0, 6.0, ((0, 16),)),
        "key_rows": scatter_about(part_splits[1], (TOKENS, HEADS * HD), 1.0, 6.0, ((0, 16),)),
        "value_rows": scatter_about(part_splits[2], (TOKENS, HEADS * HD), 1.0, 6.0, ((0, 16),)),
        "out_grad": scatter_about(part_splits[3], (TOKENS, HEADS * HD), 1.0, 6.0, ((0, 16),)),
        "doc_lengths": ragged(part_splits[4], DOCS, TOKENS, DOC_MOST, 2).astype(jnp.int32),
    }


def doc_layout(doc_lengths, base, rows):
    count = doc_lengths.shape[0]
    lengths_int = doc_lengths.astype(jnp.int32)
    starts = (jnp.cumsum(lengths_int) - lengths_int).astype(jnp.int32)
    finish = (starts + lengths_int).astype(jnp.int32)
    positions = (base + jnp.arange(rows, dtype=jnp.int32)).astype(jnp.int32)
    member = ((positions[:, None] >= starts[None, :]) & (positions[:, None] < finish[None, :])).astype(jnp.int32)
    labels = jnp.arange(count, dtype=jnp.int32)
    doc_index = lax.optimization_barrier(jnp.sum(member * labels[None, :], axis=1)).astype(jnp.int32)
    offsets = (positions - lax.optimization_barrier(jnp.sum(member * starts[None, :], axis=1))).astype(jnp.int32)
    first_doc = doc_index[0]
    last_doc = doc_index[rows - 1]
    first_start = jnp.sum(jnp.where(labels == first_doc, starts, 0))
    last_start = jnp.sum(jnp.where(labels == last_doc, starts, 0))
    first_finish = jnp.sum(jnp.where(labels == first_doc, finish, 0))
    last_finish = jnp.sum(jnp.where(labels == last_doc, finish, 0))
    carry_in = (first_start < base).astype(jnp.float32)
    reset_fwd = (last_start >= base).astype(jnp.float32)
    reset_bwd = (first_finish <= base + rows).astype(jnp.float32)
    carry_back = (last_finish > base + rows).astype(jnp.float32)
    local = jnp.arange(rows, dtype=jnp.int32)
    allowed = (doc_index[:, None] == doc_index[None, :]) & (local[:, None] >= local[None, :])
    return (offsets, doc_index == first_doc, doc_index == last_doc, carry_in, reset_fwd, reset_bwd, carry_back, allowed)

def scale_rows(offsets):
    return lax.rsqrt(offsets.astype(jnp.float32) + 1.0) * HD ** (-0.5)

def reference(query_rows, key_rows, value_rows, out_grad, doc_lengths):
    hi = lax.Precision.HIGHEST
    shape = (N_CTX, TOK_DEV, HEADS, HD)
    query_blk = query_rows.reshape(shape)
    key_blk = key_rows.reshape(shape)
    value_blk = value_rows.reshape(shape)
    grad_blk = out_grad.reshape(shape)
    block_ids = jnp.arange(N_CTX, dtype=jnp.int32)
    zero_state = jnp.zeros((HEADS, HD, HD), jnp.float32)

    def forward_step(carry, inputs):
        block_no, key_part, value_part = inputs
        layout = doc_layout(doc_lengths, block_no * TOK_DEV, TOK_DEV)
        last_rows = layout[2]
        kept = jnp.where(last_rows[:, None, None], key_part, jnp.zeros_like(key_part)).astype(jnp.float32)
        tail_state = jnp.einsum('thd,the->hde', kept, value_part.astype(jnp.float32), precision=hi)
        entering = carry * layout[3]
        return (tail_state + (1.0 - layout[4]) * carry, entering)

    def backward_step(carry, inputs):
        block_no, query_part, grad_part = inputs
        layout = doc_layout(doc_lengths, block_no * TOK_DEV, TOK_DEV)
        row_scale = scale_rows(layout[0])
        scaled = (query_part.astype(jnp.float32) * row_scale[:, None, None]).astype(jnp.bfloat16)
        kept = jnp.where(layout[1][:, None, None], scaled, jnp.zeros_like(scaled)).astype(jnp.float32)
        head_state = jnp.einsum('thd,the->hde', kept, grad_part.astype(jnp.float32), precision=hi)
        returning = carry * layout[6]
        return (head_state + (1.0 - layout[5]) * carry, returning)
    final_fwd, entering_all = lax.scan(forward_step, zero_state, (block_ids, key_blk, value_blk))
    final_bwd, returning_all = lax.scan(backward_step, zero_state, (block_ids, query_blk, grad_blk), reverse=True)

    def block_work(inputs):
        block_no, query_part, key_part, value_part, grad_part, entering, returning = inputs
        layout = doc_layout(doc_lengths, block_no * TOK_DEV, TOK_DEV)
        row_scale = scale_rows(layout[0])
        allowed = layout[7][None, :, :]
        scaled = (query_part.astype(jnp.float32) * row_scale[:, None, None]).astype(jnp.bfloat16)
        scaled_f = scaled.astype(jnp.float32)
        key_f = key_part.astype(jnp.float32)
        value_f = value_part.astype(jnp.float32)
        grad_f = grad_part.astype(jnp.float32)
        scores = jnp.einsum('thd,shd->hts', scaled_f, key_f, precision=hi)
        weights = jnp.where(allowed, scores, 0.0).astype(jnp.bfloat16).astype(jnp.float32)
        attended = jnp.einsum('thd,hde->the', scaled_f, entering, precision=hi) + jnp.einsum('hts,she->the', weights, value_f, precision=hi)
        dscores = jnp.einsum('the,she->hts', grad_f, value_f, precision=hi)
        dweights = jnp.where(allowed, dscores, 0.0).astype(jnp.bfloat16).astype(jnp.float32)
        grad_q = row_scale[:, None, None] * (jnp.einsum('the,hde->thd', grad_f, entering, precision=hi) + jnp.einsum('hts,shd->thd', dweights, key_f, precision=hi))
        grad_k = jnp.einsum('she,hde->shd', value_f, returning, precision=hi) + jnp.einsum('hts,thd->shd', dweights, scaled_f, precision=hi)
        grad_v = jnp.einsum('shd,hde->she', key_f, returning, precision=hi) + jnp.einsum('hts,the->she', weights, grad_f, precision=hi)
        return (attended.astype(jnp.bfloat16), grad_q.astype(jnp.bfloat16), grad_k.astype(jnp.bfloat16), grad_v.astype(jnp.bfloat16))
    results = lax.map(block_work, (block_ids, query_blk, key_blk, value_blk, grad_blk, entering_all, returning_all))
    flat = (TOKENS, HEADS * HD)
    return (results[0].reshape(flat), results[1].reshape(flat), results[2].reshape(flat), results[3].reshape(flat))
```

```python
import functools

import jax
import jax.numpy as jnp
from jax import lax
from jax.experimental import pallas as pl
from jax.experimental.pallas import tpu as pltpu
from jax.sharding import PartitionSpec as P

HD = 128
F32 = jnp.float32
BF16 = jnp.bfloat16
SMEM = pl.BlockSpec(memory_space=pltpu.SMEM)
VMEM = pl.BlockSpec(memory_space=pltpu.VMEM)


def cycle_within(nodes):
    return [(node, nodes[(at + 1) % len(nodes)]) for at, node in enumerate(nodes)]


def swap_pairs(count, steps):
    pairs = [(j, j + steps) for j in range(1, count - steps, 2)]
    met = {j for pair in pairs for j in pair}
    rest = [j for j in range(count) if j not in met]
    low = [j for j in rest if j < count // 2]
    high = [j for j in rest if j >= count // 2]
    groups = [low, high] if len(low) != 1 and len(high) != 1 else [rest]
    fill = [edge for group in groups for edge in cycle_within(group)]
    return pairs + [(b, a) for a, b in pairs] + fill


def ring_pairs(count, steps):
    out = []
    for j in range(count):
        target = j + steps if j % 2 else j - steps
        if not 0 <= target < count:
            target = j - 1 if j % 2 else j + 1
        out.append((j, target))
    return out


def pair_mates(count):
    return [(j, j ^ 1) for j in range(count)]


def doc_edges(lengths_ref, base, rows):
    first_start = last_start = jnp.int32(0)
    first_finish = last_finish = jnp.int32(2**30)
    start = jnp.int32(0)
    starts = []
    for doc in range(lengths_ref.shape[0]):
        finish = start + lengths_ref[doc]
        starts.append(start)
        first_start = jnp.where(start <= base, start, first_start)
        last_start = jnp.where(start < base + rows, start, last_start)
        first_finish = jnp.where(finish > base, jnp.minimum(finish, first_finish), first_finish)
        last_finish = jnp.where(finish >= base + rows, jnp.minimum(finish, last_finish), last_finish)
        start = finish
    return starts, first_start, last_start, first_finish, last_finish


def row_starts(starts, positions):
    begin = jnp.zeros_like(positions)
    for start in starts:
        begin = jnp.where(positions >= start, start, begin)
    return begin


def row_scales(starts, base, rows):
    positions = base + lax.broadcasted_iota(jnp.int32, (rows, HD), 0)
    begin = row_starts(starts, positions)
    return lax.rsqrt((positions - begin).astype(F32) + 1.0) * HD ** (-0.5)


def scale_rows(query, scales):
    heads = query.shape[1] // HD
    wide = jnp.concatenate([scales] * heads, axis=1)
    return (query.astype(F32) * wide).astype(BF16)


def dot(a, b, contract):
    return lax.dot_general(a, b, (contract, ((), ())), preferred_element_type=F32)


def states_kernel(place_ref, lengths_ref, q_ref, k_ref, v_ref, g_ref, own_ref, other_ref, gate_ref):
    rows, width = q_ref.shape
    place = place_ref[0]
    base = place * rows
    starts, _, last_start, first_finish, _ = doc_edges(lengths_ref, base, rows)
    positions = base + lax.broadcasted_iota(jnp.int32, (rows, width), 0)
    tail_keys = jnp.where(positions >= last_start, k_ref[...].astype(F32), 0.0).astype(BF16)
    tail = dot(tail_keys, v_ref[...], ((0,), (0,)))
    scaled = scale_rows(q_ref[...], row_scales(starts, base, rows)).astype(F32)
    head_rows = jnp.where(positions < first_finish, scaled, 0.0).astype(BF16)
    head = dot(head_rows, g_ref[...], ((0,), (0,)))
    odd = place % 2 == 1
    for h in range(width // HD):
        part = pl.ds(h * HD, HD)
        tail_h = tail[h * HD : (h + 1) * HD, h * HD : (h + 1) * HD]
        head_h = head[h * HD : (h + 1) * HD, h * HD : (h + 1) * HD]
        own_ref[h] = jnp.where(odd, tail_h, head_h)
        other_ref[h] = jnp.where(odd, head_h, tail_h)
    keep = jnp.where(odd, last_start < base, first_finish > base + rows)
    gate_ref[...] = jnp.full(gate_ref.shape, jnp.where(keep, 1.0, 0.0), F32)


def inner_kernel(place_ref, lengths_ref, q_ref, k_ref, v_ref, g_ref, att_ref, gq_ref, gk_ref, gv_ref):
    rows, width = q_ref.shape
    base = place_ref[0] * rows
    starts, _, _, _, _ = doc_edges(lengths_ref, base, rows)
    scaled = scale_rows(q_ref[...], row_scales(starts, base, rows))
    tile = min(256, rows)
    for at in range(0, rows, tile):
        reach = at + tile
        row_at = lax.broadcasted_iota(jnp.int32, (tile, reach), 0) + at
        column_at = lax.broadcasted_iota(jnp.int32, (tile, reach), 1)
        begin = row_starts(starts, base + row_at) - base
        allowed = (column_at <= row_at) & (column_at >= begin)
        for h in range(width // HD):
            part = slice(h * HD, (h + 1) * HD)
            scaled_t = scaled[at:reach, part]
            grad_t = g_ref[at:reach, part]
            keys = k_ref[:reach, part]
            values = v_ref[:reach, part]
            scores = dot(scaled_t, keys, ((1,), (1,)))
            weights = jnp.where(allowed, scores, 0.0).astype(BF16)
            dscores = dot(grad_t, values, ((1,), (1,)))
            dweights = jnp.where(allowed, dscores, 0.0).astype(BF16)
            att_ref[at:reach, part] = dot(weights, values, ((1,), (0,)))
            gq_ref[at:reach, part] = dot(dweights, keys, ((1,), (0,)))
            grad_k = dot(dweights, scaled_t, ((0,), (0,)))
            grad_v = dot(weights, grad_t, ((0,), (0,)))
            if at:
                gk_ref[:at, part] += grad_k[:at]
                gv_ref[:at, part] += grad_v[:at]
            gk_ref[at:reach, part] = grad_k[at:]
            gv_ref[at:reach, part] = grad_v[at:]


def split_dot(rows, state, contract):
    high = state.astype(BF16)
    low = (state - high.astype(F32)).astype(BF16)
    return dot(rows, high, contract) + dot(rows, low, contract)


def outer_kernel(slots, place_ref, lengths_ref, q_ref, k_ref, v_ref, g_ref, *refs):
    inner_refs, slot_refs, out_refs = refs[:4], refs[4 : 4 + len(slots)], refs[4 + len(slots) :]
    rows, width = q_ref.shape
    place = place_ref[0]
    base = place * rows
    starts, first_start, _, _, last_finish = doc_edges(lengths_ref, base, rows)
    odd = place % 2 == 1
    gates = []
    for steps, odd_forward in slots:
        forward = odd if odd_forward else jnp.logical_not(odd)
        before = forward & (first_start < (place - steps + 1) * rows)
        after = jnp.logical_not(forward) & (last_finish > (place + steps) * rows)
        gates.append((jnp.where(before, 1.0, 0.0), jnp.where(after, 1.0, 0.0)))
    scales = row_scales(starts, base, rows)
    scaled = scale_rows(q_ref[...], scales)
    for h in range(width // HD):
        part = slice(h * HD, (h + 1) * HD)
        entering = returning = jnp.zeros((HD, HD), F32)
        for (before, after), slot_ref in zip(gates, slot_refs):
            received = slot_ref[h]
            entering = entering + before * received
            returning = returning + after * received
        attended = inner_refs[0][:, part] + split_dot(scaled[:, part], entering, ((1,), (0,)))
        grad_q = inner_refs[1][:, part] + split_dot(g_ref[:, part], entering, ((1,), (1,)))
        grad_k = inner_refs[2][:, part] + split_dot(v_ref[:, part], returning, ((1,), (1,)))
        grad_v = inner_refs[3][:, part] + split_dot(k_ref[:, part], returning, ((1,), (0,)))
        out_refs[0][:, part] = attended.astype(BF16)
        out_refs[1][:, part] = (scales * grad_q).astype(BF16)
        out_refs[2][:, part] = grad_k.astype(BF16)
        out_refs[3][:, part] = grad_v.astype(BF16)


def body(query_rows, key_rows, value_rows, out_grad, doc_lengths):
    rows, width = query_rows.shape
    heads = width // HD
    count = lax.axis_size("ctx")
    reach = count // 4
    place = lax.axis_index("ctx").astype(jnp.int32).reshape(1)
    tensors = (query_rows, key_rows, value_rows, out_grad)
    params = pltpu.CompilerParams(vmem_limit_bytes=32 * 2**20)
    state = jax.ShapeDtypeStruct((heads, HD, HD), F32)
    own, other, gate = pl.pallas_call(
        states_kernel,
        out_shape=(state, state, jax.ShapeDtypeStruct((1, HD), F32)),
        in_specs=[SMEM, SMEM] + [VMEM] * 4,
        out_specs=[VMEM] * 3,
        compiler_params=params,
        cost_estimate=pl.CostEstimate(flops=2 * 2 * rows * width * width, bytes_accessed=4 * rows * width * 2, transcendentals=0),
        name="block_states",
    )(place, doc_lengths, *tensors)

    def send(value, pairs):
        return lax.ppermute(value, "ctx", pairs)

    mate = send(other, pair_mates(count))
    far = send(own, ring_pairs(count, reach))
    joined = own + gate[None] * mate
    slots = [(1, True), (reach, True)]
    received = [mate, far]
    for steps in range(reach - 1, 0, -1):
        pairs = swap_pairs(count, steps) if steps % 2 else ring_pairs(count, steps)
        slots.append((steps, steps % 2 == 0))
        received.append(send(joined, pairs))
    partial = jax.ShapeDtypeStruct((rows, width), F32)
    inner = pl.pallas_call(
        inner_kernel,
        out_shape=(partial,) * 4,
        in_specs=[SMEM, SMEM] + [VMEM] * 4,
        out_specs=[VMEM] * 4,
        compiler_params=params,
        cost_estimate=pl.CostEstimate(flops=6 * 2 * rows * rows * width, bytes_accessed=4 * rows * width * 6, transcendentals=0),
        name="within_block",
    )(place, doc_lengths, *tensors)
    out = jax.ShapeDtypeStruct((rows, width), BF16)
    return pl.pallas_call(
        functools.partial(outer_kernel, tuple(slots)),
        out_shape=(out,) * 4,
        in_specs=[SMEM, SMEM] + [VMEM] * (8 + len(slots)),
        out_specs=[VMEM] * 4,
        compiler_params=params,
        cost_estimate=pl.CostEstimate(flops=4 * 2 * rows * width * HD, bytes_accessed=4 * rows * width * 8, transcendentals=0),
        name="across_blocks",
    )(place, doc_lengths, *tensors, *inner, *received)


def solution(mesh):
    in_specs = (P("ctx", "head"), P("ctx", "head"), P("ctx", "head"), P("ctx", "head"), P("head"))
    out_specs = (P("ctx", "head"), P("ctx", "head"), P("ctx", "head"), P("ctx", "head"))
    return jax.shard_map(body, mesh=mesh, in_specs=in_specs, out_specs=out_specs, check_vma=False)
```

```python
import functools

import jax
import jax.numpy as jnp
from jax import lax
from jax.experimental import pallas as pl
from jax.experimental.pallas import tpu as pltpu
from jax.sharding import PartitionSpec as P

HD = 128
F32 = jnp.float32
BF16 = jnp.bfloat16
HBM = pl.BlockSpec(memory_space=pltpu.HBM)
VMEM = pl.BlockSpec(memory_space=pltpu.VMEM)


def cycle_within(nodes):
    return [(node, nodes[(at + 1) % len(nodes)]) for at, node in enumerate(nodes)]


def swap_pairs(count, steps):
    pairs = [(j, j + steps) for j in range(1, count - steps, 2)]
    met = {j for pair in pairs for j in pair}
    rest = [j for j in range(count) if j not in met]
    low = [j for j in rest if j < count // 2]
    high = [j for j in rest if j >= count // 2]
    groups = [low, high] if len(low) != 1 and len(high) != 1 else [rest]
    fill = [edge for group in groups for edge in cycle_within(group)]
    return pairs + [(b, a) for a, b in pairs] + fill


def ring_pairs(count, steps):
    out = []
    for j in range(count):
        target = j + steps if j % 2 else j - steps
        if not 0 <= target < count:
            target = j - 1 if j % 2 else j + 1
        out.append((j, target))
    return out


def pair_mates(count):
    return [(j, j ^ 1) for j in range(count)]


def doc_edges(lengths_ref, base, rows):
    first_start = last_start = jnp.int32(0)
    first_finish = last_finish = jnp.int32(2**30)
    start = jnp.int32(0)
    starts = []
    for doc in range(lengths_ref.shape[0]):
        finish = start + lengths_ref[doc]
        starts.append(start)
        first_start = jnp.where(start <= base, start, first_start)
        last_start = jnp.where(start < base + rows, start, last_start)
        first_finish = jnp.where(finish > base, jnp.minimum(finish, first_finish), first_finish)
        last_finish = jnp.where(finish >= base + rows, jnp.minimum(finish, last_finish), last_finish)
        start = finish
    return starts, first_start, last_start, first_finish, last_finish


def row_begins(starts, base, rows):
    local = lax.broadcasted_iota(jnp.int32, (rows, HD), 0)
    begin = jnp.full((rows, HD), -base, jnp.int32)
    for start in starts:
        begin = jnp.where(local >= start - base, start - base, begin)
    return begin


def row_scales(begin):
    local = lax.broadcasted_iota(jnp.int32, begin.shape, 0)
    return lax.rsqrt((local - begin).astype(F32) + 1.0) * HD ** (-0.5)


def scale_rows(query, scales):
    heads = query.shape[1] // HD
    wide = jnp.concatenate([scales] * heads, axis=1)
    return (query.astype(F32) * wide).astype(BF16)


def dot(a, b, contract):
    return lax.dot_general(a, b, (contract, ((), ())), preferred_element_type=F32)


def states_kernel(
    lengths_hbm, q_hbm, k_hbm, v_hbm, g_hbm,
    own_ref, other_ref, gate_ref, begin_ref, scaled_ref, k_ref, v_ref, g_ref,
    q_ref, lengths_ref, sems,
):
    pieces = [(lengths_hbm, lengths_ref), (k_hbm, k_ref), (v_hbm, v_ref), (q_hbm, q_ref), (g_hbm, g_ref)]
    copies = [pltpu.make_async_copy(source, target, sems.at[at]) for at, (source, target) in enumerate(pieces)]
    for copy in copies:
        copy.start()
    rows, width = q_ref.shape
    place = lax.axis_index("ctx")
    base = place * rows
    copies[0].wait()
    starts, _, last_start, first_finish, _ = doc_edges(lengths_ref, base, rows)
    odd = place % 2 == 1
    keep = jnp.where(odd, last_start < base, first_finish > base + rows)
    gate_ref[...] = jnp.full(gate_ref.shape, jnp.where(keep, 1.0, 0.0), F32)
    begin = row_begins(starts, base, rows)
    begin_ref[...] = begin
    scales = row_scales(begin)
    local = lax.broadcasted_iota(jnp.int32, (rows, width), 0)
    copies[1].wait()
    tail_keys = jnp.where(local >= last_start - base, k_ref[...].astype(F32), 0.0).astype(BF16)
    copies[2].wait()
    tail = dot(tail_keys, v_ref[...], ((0,), (0,)))
    copies[3].wait()
    scaled = scale_rows(q_ref[...], scales)
    scaled_ref[...] = scaled
    head_rows = jnp.where(local < first_finish - base, scaled.astype(F32), 0.0).astype(BF16)
    copies[4].wait()
    head = dot(head_rows, g_ref[...], ((0,), (0,)))
    for h in range(width // HD):
        part = slice(h * HD, (h + 1) * HD)
        own_ref[h] = jnp.where(odd, tail[part, part], head[part, part])
        other_ref[h] = jnp.where(odd, head[part, part], tail[part, part])


def inner_kernel(
    slots, lengths_hbm, begin_ref, scaled_ref, k_ref, v_ref, g_ref,
    gates_ref, att_ref, gq_ref, gk_ref, gv_ref, lengths_ref, sem,
):
    copy = pltpu.make_async_copy(lengths_hbm, lengths_ref, sem)
    copy.start()
    rows, width = scaled_ref.shape
    copy.wait()
    place = lax.axis_index("ctx")
    base = place * rows
    _, first_start, _, _, last_finish = doc_edges(lengths_ref, base, rows)
    odd = place % 2 == 1
    gates = []
    for steps, odd_forward in slots:
        forward = odd if odd_forward else jnp.logical_not(odd)
        gates.append(forward & (first_start < (place - steps + 1) * rows))
        gates.append(jnp.logical_not(forward) & (last_finish > (place + steps) * rows))
    for at, gate in enumerate(gates):
        gates_ref[at : at + 1, :] = jnp.full((1, HD), jnp.where(gate, 1.0, 0.0), F32)
    tile = min(256, rows)
    for at in range(0, rows, tile):
        reach = at + tile
        row_at = lax.broadcasted_iota(jnp.int32, (tile, reach), 0) + at
        column_at = lax.broadcasted_iota(jnp.int32, (tile, reach), 1)
        begin = jnp.concatenate([begin_ref[at:reach, :]] * (reach // HD), axis=1)
        allowed = (column_at <= row_at) & (column_at >= begin)
        for h in range(width // HD):
            part = slice(h * HD, (h + 1) * HD)
            scaled_t = scaled_ref[at:reach, part]
            grad_t = g_ref[at:reach, part]
            keys = k_ref[:reach, part]
            values = v_ref[:reach, part]
            scores = dot(scaled_t, keys, ((1,), (1,)))
            weights = jnp.where(allowed, scores, 0.0).astype(BF16)
            dscores = dot(grad_t, values, ((1,), (1,)))
            dweights = jnp.where(allowed, dscores, 0.0).astype(BF16)
            att_ref[at:reach, part] = dot(weights, values, ((1,), (0,)))
            gq_ref[at:reach, part] = dot(dweights, keys, ((1,), (0,)))
            grad_k = dot(dweights, scaled_t, ((0,), (0,)))
            grad_v = dot(weights, grad_t, ((0,), (0,)))
            if at:
                gk_ref[:at, part] += grad_k[:at]
                gv_ref[:at, part] += grad_v[:at]
            gk_ref[at:reach, part] = grad_k[at:]
            gv_ref[at:reach, part] = grad_v[at:]


def diagonal(blocks):
    zero = jnp.zeros((HD, HD), BF16)
    rows = [
        jnp.concatenate([block.astype(BF16) if h == at else zero for h in range(len(blocks))], axis=1)
        for at, block in enumerate(blocks)
    ]
    return jnp.concatenate(rows, axis=0)


def split(blocks):
    low = [block - block.astype(BF16).astype(F32) for block in blocks]
    return diagonal(blocks), diagonal(low)


def split_dot(rows, state, contract):
    return dot(rows, state[0], contract) + dot(rows, state[1], contract)


def outer_kernel(begin_ref, scaled_ref, k_ref, v_ref, g_ref, gates_ref, *refs):
    out_hbms, out_refs, sems = refs[-9:-5], refs[-5:-1], refs[-1]
    inner_refs, slot_refs = refs[:4], refs[4:-9]
    heads = scaled_ref.shape[1] // HD
    entering = [jnp.zeros((HD, HD), F32)] * heads
    returning = [jnp.zeros((HD, HD), F32)] * heads
    for at, slot_ref in enumerate(slot_refs):
        before, after = gates_ref[2 * at : 2 * at + 1, :], gates_ref[2 * at + 1 : 2 * at + 2, :]
        entering = [state + before * slot_ref[h] for h, state in enumerate(entering)]
        returning = [state + after * slot_ref[h] for h, state in enumerate(returning)]
    entering, returning = split(entering), split(returning)
    copies = [pltpu.make_async_copy(out_refs[at], out_hbms[at], sems.at[at]) for at in range(4)]
    attended = inner_refs[0][...] + split_dot(scaled_ref[...], entering, ((1,), (0,)))
    out_refs[0][...] = attended.astype(BF16)
    copies[0].start()
    scales = jnp.concatenate([row_scales(begin_ref[...])] * heads, axis=1)
    grad_q = inner_refs[1][...] + split_dot(g_ref[...], entering, ((1,), (1,)))
    out_refs[1][...] = (scales * grad_q).astype(BF16)
    copies[1].start()
    grad_k = inner_refs[2][...] + split_dot(v_ref[...], returning, ((1,), (1,)))
    out_refs[2][...] = grad_k.astype(BF16)
    copies[2].start()
    grad_v = inner_refs[3][...] + split_dot(k_ref[...], returning, ((1,), (0,)))
    out_refs[3][...] = grad_v.astype(BF16)
    copies[3].start()
    for copy in copies:
        copy.wait()


def body(query_rows, key_rows, value_rows, out_grad, doc_lengths):
    rows, width = query_rows.shape
    heads = width // HD
    docs = doc_lengths.shape[0]
    count = lax.axis_size("ctx")
    reach = count // 4
    arguments = (doc_lengths, query_rows, key_rows, value_rows, out_grad)
    held = [pltpu.with_memory_space_constraint(x, pltpu.HBM) for x in arguments]
    params = pltpu.CompilerParams(vmem_limit_bytes=32 * 2**20)
    state = jax.ShapeDtypeStruct((heads, HD, HD), F32)
    flat = jax.ShapeDtypeStruct((rows, width), BF16)
    partial = jax.ShapeDtypeStruct((rows, width), F32)
    own, other, gate, begin, *tensors = pl.pallas_call(
        states_kernel,
        out_shape=(state, state, jax.ShapeDtypeStruct((1, HD), F32), jax.ShapeDtypeStruct((rows, HD), jnp.int32)) + (flat,) * 4,
        in_specs=[HBM] * 5,
        out_specs=[VMEM] * 8,
        scratch_shapes=[pltpu.VMEM((rows, width), BF16), pltpu.SMEM((docs,), jnp.int32), pltpu.SemaphoreType.DMA((5,))],
        compiler_params=params,
        cost_estimate=pl.CostEstimate(flops=2 * 2 * rows * width * width, bytes_accessed=4 * rows * width * 2, transcendentals=0),
        name="block_states",
    )(*held)

    def send(value, pairs):
        return lax.ppermute(value, "ctx", pairs)

    mate = send(other, pair_mates(count))
    far = send(own, ring_pairs(count, reach))
    joined = own + gate[None] * mate
    slots = [(1, True), (reach, True)]
    received = [mate, far]
    for steps in range(1, reach):
        pairs = swap_pairs(count, steps) if steps % 2 else ring_pairs(count, steps)
        slots.append((steps, steps % 2 == 0))
        received.append(send(joined, pairs))
    inner = pl.pallas_call(
        functools.partial(inner_kernel, tuple(slots)),
        out_shape=(jax.ShapeDtypeStruct((2 * len(slots), HD), F32),) + (partial,) * 4,
        in_specs=[HBM] + [VMEM] * 5,
        out_specs=[VMEM] * 5,
        scratch_shapes=[pltpu.SMEM((docs,), jnp.int32), pltpu.SemaphoreType.DMA(())],
        compiler_params=params,
        cost_estimate=pl.CostEstimate(flops=6 * 2 * rows * rows * width, bytes_accessed=4 * rows * width * 6, transcendentals=0),
        name="within_block",
    )(held[0], begin, *tensors)
    return pl.pallas_call(
        outer_kernel,
        out_shape=(flat,) * 4,
        in_specs=[VMEM] * (10 + len(slots)),
        out_specs=[HBM] * 4,
        scratch_shapes=[pltpu.VMEM((rows, width), BF16)] * 4 + [pltpu.SemaphoreType.DMA((4,))],
        compiler_params=params,
        cost_estimate=pl.CostEstimate(flops=4 * 2 * rows * width * HD, bytes_accessed=4 * rows * width * 8, transcendentals=0),
        name="across_blocks",
    )(begin, *tensors, *inner, *received)


def solution(mesh):
    in_specs = (P("ctx", "head"), P("ctx", "head"), P("ctx", "head"), P("ctx", "head"), P("head"))
    out_specs = (P("ctx", "head"), P("ctx", "head"), P("ctx", "head"), P("ctx", "head"))
    return jax.shard_map(body, mesh=mesh, in_specs=in_specs, out_specs=out_specs, check_vma=False)
```

```python
import functools

import jax
import jax.numpy as jnp
from jax import lax
from jax.experimental import pallas as pl
from jax.experimental.pallas import tpu as pltpu
from jax.sharding import PartitionSpec as P

HD = 128
F32 = jnp.float32
BF16 = jnp.bfloat16
HBM = pl.BlockSpec(memory_space=pltpu.HBM)
VMEM = pl.BlockSpec(memory_space=pltpu.VMEM)


def ring_pairs(count, steps, odd_up):
    out = []
    for j in range(count):
        target = j + steps if (j % 2 == 1) == odd_up else j - steps
        if not 0 <= target < count:
            target = j ^ 1
        out.append((j, target))
    return out


def swap_pairs(count, steps):
    pairs = [(j, j + steps) for j in range(1, count - steps, 2)]
    return pairs + [(b, a) for a, b in pairs]


def mate_pairs(count):
    return [(j, j ^ 1) for j in range(count)]


def send(value, pairs):
    blocks, groups = lax.axis_size("ctx"), lax.axis_size("head")
    spare = 1 if groups % 2 == 0 else 0
    rest = sorted(set(range(blocks)) - {a for a, _ in pairs})
    wide = [(a * groups + g, b * groups + g) for a, b in pairs for g in range(groups)]
    wide += [(a * groups + g, a * groups + (g ^ spare)) for a in rest for g in range(groups)]
    return lax.ppermute(value, ("ctx", "head"), wide)


def doc_edges(lengths_ref, base, rows):
    first_start = last_start = jnp.int32(0)
    first_finish = last_finish = jnp.int32(2**30)
    start = jnp.int32(0)
    starts = []
    for doc in range(lengths_ref.shape[0]):
        finish = start + lengths_ref[doc]
        starts.append(start)
        first_start = jnp.where(start <= base, start, first_start)
        last_start = jnp.where(start < base + rows, start, last_start)
        first_finish = jnp.where(finish > base, jnp.minimum(finish, first_finish), first_finish)
        last_finish = jnp.where(finish >= base + rows, jnp.minimum(finish, last_finish), last_finish)
        start = finish
    return starts, first_start, last_start, first_finish, last_finish


def row_begins(starts, base, rows):
    local = lax.broadcasted_iota(jnp.int32, (rows, HD), 0)
    begin = jnp.full((rows, HD), -base, jnp.int32)
    for start in starts:
        begin = jnp.where(local >= start - base, start - base, begin)
    return begin


def row_scales(begin):
    local = lax.broadcasted_iota(jnp.int32, begin.shape, 0)
    return lax.rsqrt((local - begin).astype(F32) + 1.0) * HD ** (-0.5)


def scale_rows(query, scales):
    heads = query.shape[1] // HD
    wide = jnp.concatenate([scales] * heads, axis=1)
    return (query.astype(F32) * wide).astype(BF16)


def dot(a, b, contract):
    return lax.dot_general(a, b, (contract, ((), ())), preferred_element_type=F32)


def masked_rows(rows, scales, low, high):
    wide = jnp.concatenate([scales] * (rows.shape[1] // HD), axis=1)
    local = lax.broadcasted_iota(jnp.int32, rows.shape, 0)
    return jnp.where((local >= low) & (local < high), rows.astype(F32) * wide, 0.0).astype(BF16)


def store_heads(out_ref, product):
    for h in range(out_ref.shape[0]):
        out_ref[h] = product[h * HD : (h + 1) * HD, h * HD : (h + 1) * HD]


def trade_kernel(lengths_hbm, q_hbm, k_hbm, v_hbm, g_hbm, other_ref, left_ref, right_ref, lengths_ref, sems):
    rows = left_ref.shape[0]
    place = lax.axis_index("ctx")
    odd = place % 2 == 1
    copy = pltpu.make_async_copy(lengths_hbm, lengths_ref, sems.at[0])
    copy.start()

    @pl.when(odd)
    def _():
        pltpu.make_async_copy(q_hbm, left_ref, sems.at[1]).start()
        pltpu.make_async_copy(g_hbm, right_ref, sems.at[2]).start()

    @pl.when(jnp.logical_not(odd))
    def _():
        pltpu.make_async_copy(k_hbm, left_ref, sems.at[1]).start()
        pltpu.make_async_copy(v_hbm, right_ref, sems.at[2]).start()

    base = place * rows
    copy.wait()
    starts, _, last_start, first_finish, _ = doc_edges(lengths_ref, base, rows)
    scales = jnp.where(odd, row_scales(row_begins(starts, base, rows)), 1.0)
    low = jnp.where(odd, 0, last_start - base)
    high = jnp.where(odd, first_finish - base, rows)
    pltpu.make_async_copy(q_hbm, left_ref, sems.at[1]).wait()
    left = masked_rows(left_ref[...], scales, low, high)
    pltpu.make_async_copy(g_hbm, right_ref, sems.at[2]).wait()
    store_heads(other_ref, dot(left, right_ref[...], ((0,), (0,))))


def keep_kernel(
    lengths_hbm, q_hbm, k_hbm, v_hbm, g_hbm,
    own_ref, gate_ref, begin_ref, scaled_ref, k_ref, v_ref, g_ref,
    q_ref, lengths_ref, sems,
):
    pieces = [(lengths_hbm, lengths_ref), (q_hbm, q_ref), (k_hbm, k_ref), (v_hbm, v_ref), (g_hbm, g_ref)]
    copies = [pltpu.make_async_copy(source, target, sems.at[at]) for at, (source, target) in enumerate(pieces)]
    for copy in copies:
        copy.start()
    rows = q_ref.shape[0]
    place = lax.axis_index("ctx")
    base = place * rows
    odd = place % 2 == 1
    copies[0].wait()
    starts, _, last_start, first_finish, _ = doc_edges(lengths_ref, base, rows)
    keep = jnp.where(odd, last_start < base, first_finish > base + rows)
    gate_ref[...] = jnp.full(gate_ref.shape, jnp.where(keep, 1.0, 0.0), F32)
    begin = row_begins(starts, base, rows)
    begin_ref[...] = begin
    scales = row_scales(begin)
    copies[1].wait()
    scaled_ref[...] = scale_rows(q_ref[...], scales)
    for copy in copies[2:]:
        copy.wait()

    @pl.when(odd)
    def _():
        left = masked_rows(k_ref[...], jnp.ones_like(scales), last_start - base, rows)
        store_heads(own_ref, dot(left, v_ref[...], ((0,), (0,))))

    @pl.when(jnp.logical_not(odd))
    def _():
        left = masked_rows(scaled_ref[...], jnp.ones_like(scales), 0, first_finish - base)
        store_heads(own_ref, dot(left, g_ref[...], ((0,), (0,))))


def inner_kernel(
    slots, lengths_hbm, begin_ref, scaled_ref, k_ref, v_ref, g_ref,
    gates_ref, att_ref, gq_ref, gk_ref, gv_ref, lengths_ref, sem,
):
    copy = pltpu.make_async_copy(lengths_hbm, lengths_ref, sem)
    copy.start()
    rows, width = scaled_ref.shape
    copy.wait()
    place = lax.axis_index("ctx")
    base = place * rows
    _, first_start, _, _, last_finish = doc_edges(lengths_ref, base, rows)
    odd = place % 2 == 1
    gates = []
    for steps, odd_forward in slots:
        forward = odd if odd_forward else jnp.logical_not(odd)
        gates.append(forward & (first_start < (place - steps + 1) * rows))
        gates.append(jnp.logical_not(forward) & (last_finish > (place + steps) * rows))
    for at, gate in enumerate(gates):
        gates_ref[at : at + 1, :] = jnp.full((1, HD), jnp.where(gate, 1.0, 0.0), F32)
    tile = min(256, rows)
    for at in range(0, rows, tile):
        reach = at + tile
        row_at = lax.broadcasted_iota(jnp.int32, (tile, reach), 0) + at
        column_at = lax.broadcasted_iota(jnp.int32, (tile, reach), 1)
        begin = jnp.concatenate([begin_ref[at:reach, :]] * (reach // HD), axis=1)
        allowed = (column_at <= row_at) & (column_at >= begin)
        for h in range(width // HD):
            part = slice(h * HD, (h + 1) * HD)
            scaled_t = scaled_ref[at:reach, part]
            grad_t = g_ref[at:reach, part]
            keys = k_ref[:reach, part]
            values = v_ref[:reach, part]
            scores = dot(scaled_t, keys, ((1,), (1,)))
            weights = jnp.where(allowed, scores, 0.0).astype(BF16)
            dscores = dot(grad_t, values, ((1,), (1,)))
            dweights = jnp.where(allowed, dscores, 0.0).astype(BF16)
            att_ref[at:reach, part] = dot(weights, values, ((1,), (0,)))
            gq_ref[at:reach, part] = dot(dweights, keys, ((1,), (0,)))
            grad_k = dot(dweights, scaled_t, ((0,), (0,)))
            grad_v = dot(weights, grad_t, ((0,), (0,)))
            if at:
                gk_ref[:at, part] += grad_k[:at]
                gv_ref[:at, part] += grad_v[:at]
            gk_ref[at:reach, part] = grad_k[at:]
            gv_ref[at:reach, part] = grad_v[at:]


def diagonal(blocks):
    zero = jnp.zeros((HD, HD), BF16)
    rows = [
        jnp.concatenate([block.astype(BF16) if h == at else zero for h in range(len(blocks))], axis=1)
        for at, block in enumerate(blocks)
    ]
    return jnp.concatenate(rows, axis=0)


def split(blocks):
    low = [block - block.astype(BF16).astype(F32) for block in blocks]
    return diagonal(blocks), diagonal(low)


def split_dot(rows, state, contract):
    return dot(rows, state[0], contract) + dot(rows, state[1], contract)


def outer_kernel(begin_ref, scaled_ref, k_ref, v_ref, g_ref, gates_ref, *refs):
    out_hbms, out_refs, sems = refs[-9:-5], refs[-5:-1], refs[-1]
    inner_refs, slot_refs = refs[:4], refs[4:-9]
    heads = scaled_ref.shape[1] // HD
    entering = [jnp.zeros((HD, HD), F32)] * heads
    returning = [jnp.zeros((HD, HD), F32)] * heads
    for at, slot_ref in enumerate(slot_refs):
        before, after = gates_ref[2 * at : 2 * at + 1, :], gates_ref[2 * at + 1 : 2 * at + 2, :]
        entering = [state + before * slot_ref[h] for h, state in enumerate(entering)]
        returning = [state + after * slot_ref[h] for h, state in enumerate(returning)]
    entering, returning = split(entering), split(returning)
    copies = [pltpu.make_async_copy(out_refs[at], out_hbms[at], sems.at[at]) for at in range(4)]
    attended = inner_refs[0][...] + split_dot(scaled_ref[...], entering, ((1,), (0,)))
    out_refs[0][...] = attended.astype(BF16)
    copies[0].start()
    scales = jnp.concatenate([row_scales(begin_ref[...])] * heads, axis=1)
    grad_q = inner_refs[1][...] + split_dot(g_ref[...], entering, ((1,), (1,)))
    out_refs[1][...] = (scales * grad_q).astype(BF16)
    copies[1].start()
    grad_k = inner_refs[2][...] + split_dot(v_ref[...], returning, ((1,), (1,)))
    out_refs[2][...] = grad_k.astype(BF16)
    copies[2].start()
    grad_v = inner_refs[3][...] + split_dot(k_ref[...], returning, ((1,), (0,)))
    out_refs[3][...] = grad_v.astype(BF16)
    copies[3].start()
    for copy in copies:
        copy.wait()


def body(query_rows, key_rows, value_rows, out_grad, doc_lengths):
    rows, width = query_rows.shape
    heads = width // HD
    docs = doc_lengths.shape[0]
    count = lax.axis_size("ctx")
    reach = count // 4
    arguments = (doc_lengths, query_rows, key_rows, value_rows, out_grad)
    held = [pltpu.with_memory_space_constraint(x, pltpu.HBM) for x in arguments]
    params = pltpu.CompilerParams(vmem_limit_bytes=32 * 2**20)
    state = jax.ShapeDtypeStruct((heads, HD, HD), F32)
    flat = jax.ShapeDtypeStruct((rows, width), BF16)
    partial = jax.ShapeDtypeStruct((rows, width), F32)
    fetch = [pltpu.VMEM((rows, width), BF16), pltpu.SMEM((docs,), jnp.int32), pltpu.SemaphoreType.DMA((5,))]
    other = pl.pallas_call(
        trade_kernel,
        out_shape=state,
        in_specs=[HBM] * 5,
        out_specs=VMEM,
        scratch_shapes=[pltpu.VMEM((rows, width), BF16)] + fetch,
        compiler_params=params,
        cost_estimate=pl.CostEstimate(flops=2 * rows * width * width, bytes_accessed=2 * rows * width * 2, transcendentals=0),
        name="traded_state",
    )(*held)
    mate = send(other, mate_pairs(count))
    own, gate, begin, *tensors = pl.pallas_call(
        keep_kernel,
        out_shape=(state, jax.ShapeDtypeStruct((1, HD), F32), jax.ShapeDtypeStruct((rows, HD), jnp.int32)) + (flat,) * 4,
        in_specs=[HBM] * 5,
        out_specs=[VMEM] * 7,
        scratch_shapes=fetch,
        compiler_params=params,
        cost_estimate=pl.CostEstimate(flops=2 * rows * width * width, bytes_accessed=4 * rows * width * 4, transcendentals=0),
        name="kept_state",
    )(*held)
    far = [(reach, True, send(own, ring_pairs(count, reach, True)))]
    joined = own + gate[None] * mate
    near = [
        (steps, False, send(joined, swap_pairs(count, steps))) if steps % 2
        else (steps, True, send(joined, ring_pairs(count, steps, True)))
        for steps in (3, 1, 2)
    ]
    slots = [(1, True, mate)] + far + near
    received = [value for _, _, value in slots]
    slots = [(steps, odd_forward) for steps, odd_forward, _ in slots]
    inner = pl.pallas_call(
        functools.partial(inner_kernel, tuple(slots)),
        out_shape=(jax.ShapeDtypeStruct((2 * len(slots), HD), F32),) + (partial,) * 4,
        in_specs=[HBM] + [VMEM] * 5,
        out_specs=[VMEM] * 5,
        scratch_shapes=[pltpu.SMEM((docs,), jnp.int32), pltpu.SemaphoreType.DMA(())],
        compiler_params=params,
        cost_estimate=pl.CostEstimate(flops=6 * 2 * rows * rows * width, bytes_accessed=4 * rows * width * 6, transcendentals=0),
        name="within_block",
    )(held[0], begin, *tensors)
    return pl.pallas_call(
        outer_kernel,
        out_shape=(flat,) * 4,
        in_specs=[VMEM] * (10 + len(slots)),
        out_specs=[HBM] * 4,
        scratch_shapes=[pltpu.VMEM((rows, width), BF16)] * 4 + [pltpu.SemaphoreType.DMA((4,))],
        compiler_params=params,
        cost_estimate=pl.CostEstimate(flops=4 * 2 * rows * width * HD, bytes_accessed=4 * rows * width * 8, transcendentals=0),
        name="across_blocks",
    )(begin, *tensors, *inner, *received)


def solution(mesh):
    in_specs = (P("ctx", "head"), P("ctx", "head"), P("ctx", "head"), P("ctx", "head"), P("head"))
    out_specs = (P("ctx", "head"), P("ctx", "head"), P("ctx", "head"), P("ctx", "head"))
    return jax.shard_map(body, mesh=mesh, in_specs=in_specs, out_specs=out_specs, check_vma=False)
```

```python
import functools

import jax
import jax.numpy as jnp
from jax import lax
from jax.experimental import pallas as pl
from jax.experimental.pallas import tpu as pltpu
from jax.sharding import PartitionSpec as P

HD = 128
F32 = jnp.float32
BF16 = jnp.bfloat16
HBM = pl.BlockSpec(memory_space=pltpu.HBM)
VMEM = pl.BlockSpec(memory_space=pltpu.VMEM)


def ring_pairs(count, steps, odd_up):
    out = []
    for j in range(count):
        target = j + steps if (j % 2 == 1) == odd_up else j - steps
        if not 0 <= target < count:
            target = j ^ 1
        out.append((j, target))
    return out


def swap_pairs(count, steps):
    pairs = [(j, j + steps) for j in range(1, count - steps, 2)]
    return pairs + [(b, a) for a, b in pairs]


def group_pairs(count, steps, first):
    pairs = [(j, j + steps) for j in range(count - steps) if j // steps % 2 == first]
    return pairs + [(b, a) for a, b in pairs]


def mate_pairs(count):
    return [(j, j ^ 1) for j in range(count)]


def send(value, pairs):
    blocks, groups = lax.axis_size("ctx"), lax.axis_size("head")
    spare = 1 if groups % 2 == 0 else 0
    rest = sorted(set(range(blocks)) - {a for a, _ in pairs})
    wide = [(a * groups + g, b * groups + g) for a, b in pairs for g in range(groups)]
    wide += [(a * groups + g, a * groups + (g ^ spare)) for a in rest for g in range(groups)]
    return lax.ppermute(value, ("ctx", "head"), wide)


def doc_edges(lengths_ref, base, rows):
    first_start = last_start = jnp.int32(0)
    first_finish = last_finish = jnp.int32(2**30)
    start = jnp.int32(0)
    starts = []
    for doc in range(lengths_ref.shape[0]):
        finish = start + lengths_ref[doc]
        starts.append(start)
        first_start = jnp.where(start <= base, start, first_start)
        last_start = jnp.where(start < base + rows, start, last_start)
        first_finish = jnp.where(finish > base, jnp.minimum(finish, first_finish), first_finish)
        last_finish = jnp.where(finish >= base + rows, jnp.minimum(finish, last_finish), last_finish)
        start = finish
    return starts, first_start, last_start, first_finish, last_finish


def row_begins(starts, base, rows):
    local = lax.broadcasted_iota(jnp.int32, (rows, HD), 0)
    begin = jnp.full((rows, HD), -base, jnp.int32)
    for start in starts:
        begin = jnp.where(local >= start - base, start - base, begin)
    return begin


def row_scales(begin):
    local = lax.broadcasted_iota(jnp.int32, begin.shape, 0)
    return lax.rsqrt((local - begin).astype(F32) + 1.0) * HD ** (-0.5)


def scale_rows(query, scales):
    heads = query.shape[1] // HD
    wide = jnp.concatenate([scales] * heads, axis=1)
    return (query.astype(F32) * wide).astype(BF16)


def dot(a, b, contract):
    return lax.dot_general(a, b, (contract, ((), ())), preferred_element_type=F32)


def states_kernel(
    reach, lengths_hbm, q_hbm, k_hbm, v_hbm, g_hbm, own_ref, other_ref, even_ref, odd_ref, gate_ref, pick_ref,
    q_ref, k_ref, v_ref, g_ref, lengths_ref, sems,
):
    pieces = [(lengths_hbm, lengths_ref), (k_hbm, k_ref), (v_hbm, v_ref), (q_hbm, q_ref), (g_hbm, g_ref)]
    copies = [pltpu.make_async_copy(source, target, sems.at[at]) for at, (source, target) in enumerate(pieces)]
    for copy in copies:
        copy.start()
    rows, width = q_ref.shape
    place = lax.axis_index("ctx")
    base = place * rows
    copies[0].wait()
    starts, _, last_start, first_finish, _ = doc_edges(lengths_ref, base, rows)
    odd = place % 2 == 1
    upper = place // reach % 2 == 1
    keep = jnp.where(odd, last_start < base, first_finish > base + rows)
    gate_ref[...] = jnp.full(gate_ref.shape, jnp.where(keep, 1.0, 0.0), F32)
    at_end = (place == 0) | (place == lax.axis_size("ctx") - 1)
    for at, picked in enumerate((odd == upper, at_end)):
        pick_ref[at : at + 1, :] = jnp.full((1, HD), jnp.where(picked, 1.0, 0.0), F32)
    scales = row_scales(row_begins(starts, base, rows))
    local = lax.broadcasted_iota(jnp.int32, (rows, width), 0)
    copies[1].wait()
    tail_keys = jnp.where(local >= last_start - base, k_ref[...].astype(F32), 0.0).astype(BF16)
    copies[2].wait()
    tail = dot(tail_keys, v_ref[...], ((0,), (0,)))
    copies[3].wait()
    scaled = q_ref[...].astype(F32) * jnp.concatenate([scales] * (width // HD), axis=1)
    head_rows = jnp.where(local < first_finish - base, scaled, 0.0).astype(BF16)
    copies[4].wait()
    head = dot(head_rows, g_ref[...], ((0,), (0,)))
    for h in range(width // HD):
        part = slice(h * HD, (h + 1) * HD)
        own_ref[h] = jnp.where(odd, tail[part, part], head[part, part])
        other_ref[h] = jnp.where(odd, head[part, part], tail[part, part])
        even_ref[h] = jnp.where(upper, head[part, part], tail[part, part])
        odd_ref[h] = jnp.where(upper, tail[part, part], head[part, part])


def inner_kernel(
    slots, reach, lengths_hbm, q_hbm, k_hbm, v_hbm, g_hbm,
    gates_ref, begin_ref, scaled_ref, k_ref, v_ref, g_ref, att_ref, gq_ref, gk_ref, gv_ref,
    q_ref, lengths_ref, sems,
):
    pieces = [(lengths_hbm, lengths_ref), (q_hbm, q_ref), (k_hbm, k_ref), (v_hbm, v_ref), (g_hbm, g_ref)]
    copies = [pltpu.make_async_copy(source, target, sems.at[at]) for at, (source, target) in enumerate(pieces)]
    for copy in copies:
        copy.start()
    rows, width = scaled_ref.shape
    place = lax.axis_index("ctx")
    base = place * rows
    odd = place % 2 == 1
    upper = place // reach % 2 == 1
    copies[0].wait()
    starts, first_start, _, _, last_finish = doc_edges(lengths_ref, base, rows)
    even, lower = jnp.logical_not(odd), jnp.logical_not(upper)
    kinds = {"odd": odd, "ring": odd, "even": even, "relay": even, "upper": upper, "lower": lower}
    by_end = (place == 1) | (place == lax.axis_size("ctx") - 2)

    def gate_of(steps, kind):
        forward = kinds[kind]
        before = forward & (first_start < (place - steps + 1) * rows)
        after = jnp.logical_not(forward) & (last_finish > (place + steps) * rows)
        return before, after

    for at, (steps, kind) in enumerate(slots):
        before, after = gate_of(steps, kind)
        if kind == "relay":
            before, after = before & jnp.logical_not(by_end), after & jnp.logical_not(by_end)
        if kind == "ring":
            far_before, far_after = gate_of(reach - 1, "relay")
            before, after = before | (by_end & far_before), after | (by_end & far_after)
        gates_ref[2 * at : 2 * at + 1, :] = jnp.full((1, HD), jnp.where(before, 1.0, 0.0), F32)
        gates_ref[2 * at + 1 : 2 * at + 2, :] = jnp.full((1, HD), jnp.where(after, 1.0, 0.0), F32)
    begin_rows = row_begins(starts, base, rows)
    begin_ref[...] = begin_rows
    copies[1].wait()
    scaled_ref[...] = scale_rows(q_ref[...], row_scales(begin_rows))
    for copy in copies[2:]:
        copy.wait()
    tile = min(256, rows)
    for at in range(0, rows, tile):
        reach = at + tile
        row_at = lax.broadcasted_iota(jnp.int32, (tile, reach), 0) + at
        column_at = lax.broadcasted_iota(jnp.int32, (tile, reach), 1)
        begin = jnp.concatenate([begin_ref[at:reach, :]] * (reach // HD), axis=1)
        allowed = (column_at <= row_at) & (column_at >= begin)
        for h in range(width // HD):
            part = slice(h * HD, (h + 1) * HD)
            scaled_t = scaled_ref[at:reach, part]
            grad_t = g_ref[at:reach, part]
            keys = k_ref[:reach, part]
            values = v_ref[:reach, part]
            scores = dot(scaled_t, keys, ((1,), (1,)))
            weights = jnp.where(allowed, scores, 0.0).astype(BF16)
            dscores = dot(grad_t, values, ((1,), (1,)))
            dweights = jnp.where(allowed, dscores, 0.0).astype(BF16)
            att_ref[at:reach, part] = dot(weights, values, ((1,), (0,)))
            gq_ref[at:reach, part] = dot(dweights, keys, ((1,), (0,)))
            grad_k = dot(dweights, scaled_t, ((0,), (0,)))
            grad_v = dot(weights, grad_t, ((0,), (0,)))
            if at:
                gk_ref[:at, part] += grad_k[:at]
                gv_ref[:at, part] += grad_v[:at]
            gk_ref[at:reach, part] = grad_k[at:]
            gv_ref[at:reach, part] = grad_v[at:]


def diagonal(blocks):
    zero = jnp.zeros((HD, HD), BF16)
    rows = [
        jnp.concatenate([block.astype(BF16) if h == at else zero for h in range(len(blocks))], axis=1)
        for at, block in enumerate(blocks)
    ]
    return jnp.concatenate(rows, axis=0)


def split(blocks):
    low = [block - block.astype(BF16).astype(F32) for block in blocks]
    return diagonal(blocks), diagonal(low)


def split_dot(rows, state, contract):
    return dot(rows, state[0], contract) + dot(rows, state[1], contract)


def outer_kernel(gates_ref, begin_ref, scaled_ref, k_ref, v_ref, g_ref, *refs):
    out_hbms, out_refs, sems = refs[-9:-5], refs[-5:-1], refs[-1]
    inner_refs, slot_refs = refs[:4], refs[4:-9]
    heads = scaled_ref.shape[1] // HD
    entering = [jnp.zeros((HD, HD), F32)] * heads
    returning = [jnp.zeros((HD, HD), F32)] * heads
    for at, slot_ref in enumerate(slot_refs):
        before, after = gates_ref[2 * at : 2 * at + 1, :], gates_ref[2 * at + 1 : 2 * at + 2, :]
        entering = [state + before * slot_ref[h] for h, state in enumerate(entering)]
        returning = [state + after * slot_ref[h] for h, state in enumerate(returning)]
    entering, returning = split(entering), split(returning)
    copies = [pltpu.make_async_copy(out_refs[at], out_hbms[at], sems.at[at]) for at in range(4)]
    attended = inner_refs[0][...] + split_dot(scaled_ref[...], entering, ((1,), (0,)))
    out_refs[0][...] = attended.astype(BF16)
    copies[0].start()
    scales = jnp.concatenate([row_scales(begin_ref[...])] * heads, axis=1)
    grad_q = inner_refs[1][...] + split_dot(g_ref[...], entering, ((1,), (1,)))
    out_refs[1][...] = (scales * grad_q).astype(BF16)
    copies[1].start()
    grad_k = inner_refs[2][...] + split_dot(v_ref[...], returning, ((1,), (1,)))
    out_refs[2][...] = grad_k.astype(BF16)
    copies[2].start()
    grad_v = inner_refs[3][...] + split_dot(k_ref[...], returning, ((1,), (0,)))
    out_refs[3][...] = grad_v.astype(BF16)
    copies[3].start()
    for copy in copies:
        copy.wait()


def body(query_rows, key_rows, value_rows, out_grad, doc_lengths):
    rows, width = query_rows.shape
    heads = width // HD
    docs = doc_lengths.shape[0]
    count = lax.axis_size("ctx")
    reach = count // 4
    arguments = (doc_lengths, query_rows, key_rows, value_rows, out_grad)
    held = [pltpu.with_memory_space_constraint(x, pltpu.HBM) for x in arguments]
    params = pltpu.CompilerParams(vmem_limit_bytes=32 * 2**20)
    state = jax.ShapeDtypeStruct((heads, HD, HD), F32)
    flat = jax.ShapeDtypeStruct((rows, width), BF16)
    partial = jax.ShapeDtypeStruct((rows, width), F32)
    fetch = [pltpu.SMEM((docs,), jnp.int32), pltpu.SemaphoreType.DMA((5,))]
    own, other, even, odd, gate, pick = pl.pallas_call(
        functools.partial(states_kernel, reach),
        out_shape=(state,) * 4 + (jax.ShapeDtypeStruct((1, HD), F32), jax.ShapeDtypeStruct((2, HD), F32)),
        in_specs=[HBM] * 5,
        out_specs=[VMEM] * 6,
        scratch_shapes=[pltpu.VMEM((rows, width), BF16)] * 4 + fetch,
        compiler_params=params,
        cost_estimate=pl.CostEstimate(flops=2 * 2 * rows * width * width, bytes_accessed=4 * rows * width * 2, transcendentals=0),
        name="block_states",
    )(*held)
    mate = send(other, mate_pairs(count))
    far = [
        (reach, "upper", send(even, group_pairs(count, reach, 0))),
        (reach, "lower", send(odd, group_pairs(count, reach, 1))),
    ]
    joined = own + gate[None] * mate
    ringed = jnp.where(pick[1] > 0.5, far[0][2], joined)
    high_far, _ = lax.optimization_barrier((far[1][2], ringed))
    relayed = jnp.where(pick[0] > 0.5, far[0][2], high_far)
    near = [
        (reach - 1, "relay", send(relayed, mate_pairs(count)[2:-2])),
        (2, "ring", send(ringed, ring_pairs(count, 2, True))),
        *[(steps, "odd", send(joined, ring_pairs(count, steps, True))) for steps in range(4, reach - 1, 2)],
        *[(steps, "even", send(joined, swap_pairs(count, steps))) for steps in range(1, reach - 1, 2)],
    ]
    slots = [(1, "odd", mate)] + far + near
    received = [value for _, _, value in slots]
    slots = [(steps, kind) for steps, kind, _ in slots]
    gates, begin, *tensors = pl.pallas_call(
        functools.partial(inner_kernel, tuple(slots), reach),
        out_shape=(jax.ShapeDtypeStruct((2 * len(slots), HD), F32), jax.ShapeDtypeStruct((rows, HD), jnp.int32))
        + (flat,) * 4
        + (partial,) * 4,
        in_specs=[HBM] * 5,
        out_specs=[VMEM] * 10,
        scratch_shapes=[pltpu.VMEM((rows, width), BF16)] + fetch,
        compiler_params=params,
        cost_estimate=pl.CostEstimate(flops=6 * 2 * rows * rows * width, bytes_accessed=4 * rows * width * 6, transcendentals=0),
        name="within_block",
    )(*held)
    return pl.pallas_call(
        outer_kernel,
        out_shape=(flat,) * 4,
        in_specs=[VMEM] * (10 + len(slots)),
        out_specs=[HBM] * 4,
        scratch_shapes=[pltpu.VMEM((rows, width), BF16)] * 4 + [pltpu.SemaphoreType.DMA((4,))],
        compiler_params=params,
        cost_estimate=pl.CostEstimate(flops=4 * 2 * rows * width * HD, bytes_accessed=4 * rows * width * 8, transcendentals=0),
        name="across_blocks",
    )(gates, begin, *tensors, *received)


def solution(mesh):
    in_specs = (P("ctx", "head"), P("ctx", "head"), P("ctx", "head"), P("ctx", "head"), P("head"))
    out_specs = (P("ctx", "head"), P("ctx", "head"), P("ctx", "head"), P("ctx", "head"))
    return jax.shard_map(body, mesh=mesh, in_specs=in_specs, out_specs=out_specs, check_vma=False)
```

```python
import functools

import jax
import jax.numpy as jnp
from jax import lax
from jax.experimental import pallas as pl
from jax.experimental.pallas import tpu as pltpu
from jax.sharding import PartitionSpec as P

HD = 128
F32 = jnp.float32
BF16 = jnp.bfloat16
HBM = pl.BlockSpec(memory_space=pltpu.HBM)
VMEM = pl.BlockSpec(memory_space=pltpu.VMEM)


def ring_pairs(count, steps, odd_up):
    out = []
    for j in range(count):
        target = j + steps if (j % 2 == 1) == odd_up else j - steps
        if not 0 <= target < count:
            target = j ^ 1
        out.append((j, target))
    return out


def swap_pairs(count, steps):
    pairs = [(j, j + steps) for j in range(1, count - steps, 2)]
    return pairs + [(b, a) for a, b in pairs]


def group_pairs(count, steps, first):
    pairs = [(j, j + steps) for j in range(count - steps) if j // steps % 2 == first]
    return pairs + [(b, a) for a, b in pairs]


def mate_pairs(count):
    return [(j, j ^ 1) for j in range(count)]


def send(value, pairs):
    blocks, groups = lax.axis_size("ctx"), lax.axis_size("head")
    spare = 1 if groups % 2 == 0 else 0
    rest = sorted(set(range(blocks)) - {a for a, _ in pairs})
    wide = [(a * groups + g, b * groups + g) for a, b in pairs for g in range(groups)]
    wide += [(a * groups + g, a * groups + (g ^ spare)) for a in rest for g in range(groups)]
    return lax.ppermute(value, ("ctx", "head"), wide)


def doc_edges(lengths_ref, base, rows):
    first_start = last_start = jnp.int32(0)
    first_finish = last_finish = jnp.int32(2**30)
    start = jnp.int32(0)
    starts = []
    for doc in range(lengths_ref.shape[0]):
        finish = start + lengths_ref[doc]
        starts.append(start)
        first_start = jnp.where(start <= base, start, first_start)
        last_start = jnp.where(start < base + rows, start, last_start)
        first_finish = jnp.where(finish > base, jnp.minimum(finish, first_finish), first_finish)
        last_finish = jnp.where(finish >= base + rows, jnp.minimum(finish, last_finish), last_finish)
        start = finish
    return starts, first_start, last_start, first_finish, last_finish


def row_begins(starts, base, rows):
    local = lax.broadcasted_iota(jnp.int32, (rows, HD), 0)
    begin = jnp.full((rows, HD), -base, jnp.int32)
    for start in starts:
        begin = jnp.where(local >= start - base, start - base, begin)
    return begin


def row_scales(begin):
    local = lax.broadcasted_iota(jnp.int32, begin.shape, 0)
    return lax.rsqrt((local - begin).astype(F32) + 1.0) * HD ** (-0.5)


def dot(a, b, contract):
    return lax.dot_general(a, b, (contract, ((), ())), preferred_element_type=F32)


def scaled_rows(rows, weights):
    return (rows.astype(F32) * jnp.concatenate([weights] * (rows.shape[1] // HD), axis=1)).astype(BF16)


def store_product(out_ref, left, right):
    for h in range(out_ref.shape[0]):
        part = slice(h * HD, (h + 1) * HD)
        out_ref[h] = dot(left[:, part], right[:, part], ((0,), (0,)))


def gate_of(place, rows, ends, steps, forward):
    _, first_start, _, _, last_finish = ends
    before = forward & (first_start < (place - steps + 1) * rows)
    after = jnp.logical_not(forward) & (last_finish > (place + steps) * rows)
    return before, after


def store_flags(out_ref, flags):
    for at, flag in enumerate(flags):
        out_ref[at : at + 1, :] = jnp.full((1, HD), jnp.where(flag, 1.0, 0.0), F32)


def trade_kernel(
    slots, reach, lengths_hbm, q_hbm, k_hbm, v_hbm, g_hbm,
    other_ref, left_ref, right_ref, own_left_ref, own_right_ref, weight_ref, begin_ref, flags_ref, gates_ref,
    lengths_ref, sems,
):
    rows = left_ref.shape[0]
    place = lax.axis_index("ctx")
    odd = place % 2 == 1
    lengths_copy = pltpu.make_async_copy(lengths_hbm, lengths_ref, sems.at[0])
    lengths_copy.start()
    targets = (left_ref, right_ref, own_left_ref, own_right_ref)

    def fetch(*sources):
        return [pltpu.make_async_copy(a, b, sems.at[1 + at]) for at, (a, b) in enumerate(zip(sources, targets))]

    @pl.when(odd)
    def _():
        for copy in fetch(q_hbm, g_hbm, k_hbm, v_hbm):
            copy.start()

    @pl.when(jnp.logical_not(odd))
    def _():
        for copy in fetch(k_hbm, v_hbm, q_hbm, g_hbm):
            copy.start()

    copies = fetch(q_hbm, g_hbm, k_hbm, v_hbm)
    base = place * rows
    lengths_copy.wait()
    ends = doc_edges(lengths_ref, base, rows)
    starts, first_start, last_start, first_finish, last_finish = ends
    begin = row_begins(starts, base, rows)
    begin_ref[...] = begin
    scales = row_scales(begin)
    local = lax.broadcasted_iota(jnp.int32, begin.shape, 0)
    tail = jnp.where(local >= last_start - base, 1.0, 0.0)
    head = jnp.where(local < first_finish - base, scales, 0.0)
    weight_ref[...] = jnp.where(odd, tail, head)
    weights = jnp.where(odd, head, tail)
    even = jnp.logical_not(odd)
    upper = place // reach % 2 == 1
    lower = jnp.logical_not(upper)
    count = lax.axis_size("ctx")
    keep = jnp.where(odd, last_start < base, first_finish > base + rows)
    store_flags(flags_ref, [keep, odd == upper, (place == 0) | (place == count - 1)])
    kinds = {"odd": odd, "ring": odd, "even": even, "relay": even, "upper": upper, "lower": lower}
    by_end = (place == 1) | (place == count - 2)
    gates = []
    for steps, kind in slots:
        before, after = gate_of(place, rows, ends, steps, kinds[kind])
        if kind == "relay":
            before, after = before & jnp.logical_not(by_end), after & jnp.logical_not(by_end)
        if kind == "ring":
            far_before, far_after = gate_of(place, rows, ends, reach - 1, even)
            before, after = before | (by_end & far_before), after | (by_end & far_after)
        gates += [before, after]
    store_flags(gates_ref, gates)
    copies[0].wait()
    left = scaled_rows(left_ref[...], weights)
    copies[1].wait()
    store_product(other_ref, left, right_ref[...])
    copies[2].wait()
    copies[3].wait()


def keep_kernel(reach, left_ref, right_ref, weight_ref, other_ref, own_ref, even_ref, odd_ref):
    place = lax.axis_index("ctx")
    crossed = (place % 2 == 1) == (place // reach % 2 == 1)
    store_product(own_ref, scaled_rows(left_ref[...], weight_ref[...]), right_ref[...])
    own, other = own_ref[...], other_ref[...]
    even_ref[...] = jnp.where(crossed, other, own)
    odd_ref[...] = jnp.where(crossed, own, other)


def inner_kernel(
    left_ref, right_ref, own_left_ref, own_right_ref, begin_ref,
    scaled_ref, k_ref, v_ref, g_ref, att_ref, gq_ref, gk_ref, gv_ref,
):
    rows, width = scaled_ref.shape
    odd = lax.axis_index("ctx") % 2 == 1
    left, right, own_left, own_right = left_ref[...], right_ref[...], own_left_ref[...], own_right_ref[...]
    scaled_ref[...] = scaled_rows(jnp.where(odd, left, own_left), row_scales(begin_ref[...]))
    k_ref[...] = jnp.where(odd, own_left, left)
    v_ref[...] = jnp.where(odd, own_right, right)
    g_ref[...] = jnp.where(odd, right, own_right)
    tile = min(256, rows)
    for at in range(0, rows, tile):
        reach = at + tile
        row_at = lax.broadcasted_iota(jnp.int32, (tile, reach), 0) + at
        column_at = lax.broadcasted_iota(jnp.int32, (tile, reach), 1)
        begin = jnp.concatenate([begin_ref[at:reach, :]] * (reach // HD), axis=1)
        allowed = (column_at <= row_at) & (column_at >= begin)
        for h in range(width // HD):
            part = slice(h * HD, (h + 1) * HD)
            scaled_t = scaled_ref[at:reach, part]
            grad_t = g_ref[at:reach, part]
            keys = k_ref[:reach, part]
            values = v_ref[:reach, part]
            scores = dot(scaled_t, keys, ((1,), (1,)))
            weights = jnp.where(allowed, scores, 0.0).astype(BF16)
            dscores = dot(grad_t, values, ((1,), (1,)))
            dweights = jnp.where(allowed, dscores, 0.0).astype(BF16)
            att_ref[at:reach, part] = dot(weights, values, ((1,), (0,)))
            gq_ref[at:reach, part] = dot(dweights, keys, ((1,), (0,)))
            grad_k = dot(dweights, scaled_t, ((0,), (0,)))
            grad_v = dot(weights, grad_t, ((0,), (0,)))
            if at:
                gk_ref[:at, part] += grad_k[:at]
                gv_ref[:at, part] += grad_v[:at]
            gk_ref[at:reach, part] = grad_k[at:]
            gv_ref[at:reach, part] = grad_v[at:]


def diagonal(blocks):
    zero = jnp.zeros((HD, HD), BF16)
    rows = [
        jnp.concatenate([block.astype(BF16) if h == at else zero for h in range(len(blocks))], axis=1)
        for at, block in enumerate(blocks)
    ]
    return jnp.concatenate(rows, axis=0)


def split(blocks):
    low = [block - block.astype(BF16).astype(F32) for block in blocks]
    return diagonal(blocks), diagonal(low)


def split_dot(rows, state, contract):
    return dot(rows, state[0], contract) + dot(rows, state[1], contract)


def outer_kernel(gates_ref, begin_ref, scaled_ref, k_ref, v_ref, g_ref, *refs):
    out_hbms, out_refs, sems = refs[-9:-5], refs[-5:-1], refs[-1]
    inner_refs, slot_refs = refs[:4], refs[4:-9]
    heads = scaled_ref.shape[1] // HD
    entering = [jnp.zeros((HD, HD), F32)] * heads
    returning = [jnp.zeros((HD, HD), F32)] * heads
    for at, slot_ref in enumerate(slot_refs):
        before, after = gates_ref[2 * at : 2 * at + 1, :], gates_ref[2 * at + 1 : 2 * at + 2, :]
        entering = [state + before * slot_ref[h] for h, state in enumerate(entering)]
        returning = [state + after * slot_ref[h] for h, state in enumerate(returning)]
    entering, returning = split(entering), split(returning)
    copies = [pltpu.make_async_copy(out_refs[at], out_hbms[at], sems.at[at]) for at in range(4)]
    attended = inner_refs[0][...] + split_dot(scaled_ref[...], entering, ((1,), (0,)))
    out_refs[0][...] = attended.astype(BF16)
    copies[0].start()
    scales = jnp.concatenate([row_scales(begin_ref[...])] * heads, axis=1)
    grad_q = inner_refs[1][...] + split_dot(g_ref[...], entering, ((1,), (1,)))
    out_refs[1][...] = (scales * grad_q).astype(BF16)
    copies[1].start()
    grad_k = inner_refs[2][...] + split_dot(v_ref[...], returning, ((1,), (1,)))
    out_refs[2][...] = grad_k.astype(BF16)
    copies[2].start()
    grad_v = inner_refs[3][...] + split_dot(k_ref[...], returning, ((1,), (0,)))
    out_refs[3][...] = grad_v.astype(BF16)
    copies[3].start()
    for copy in copies:
        copy.wait()


def body(query_rows, key_rows, value_rows, out_grad, doc_lengths):
    rows, width = query_rows.shape
    heads = width // HD
    docs = doc_lengths.shape[0]
    count = lax.axis_size("ctx")
    reach = count // 4
    arguments = (doc_lengths, query_rows, key_rows, value_rows, out_grad)
    held = [pltpu.with_memory_space_constraint(x, pltpu.HBM) for x in arguments]
    params = pltpu.CompilerParams(vmem_limit_bytes=32 * 2**20)
    state = jax.ShapeDtypeStruct((heads, HD, HD), F32)
    flat = jax.ShapeDtypeStruct((rows, width), BF16)
    partial = jax.ShapeDtypeStruct((rows, width), F32)
    kinds = [(1, "odd"), (reach, "upper"), (reach, "lower")] + [(reach - 1, "relay")] + [(2, "ring")] + [(steps, "odd") for steps in range(4, reach - 1, 2)] + [(steps, "even") for steps in range(1, reach - 1, 2)]
    rows_of = lambda n, kind: jax.ShapeDtypeStruct((n, HD), kind)
    other, left, right, own_left, own_right, weight, begin, flags, gates = pl.pallas_call(
        functools.partial(trade_kernel, tuple(kinds), reach),
        out_shape=(state,) + (flat,) * 4 + (rows_of(rows, F32), rows_of(rows, jnp.int32), rows_of(3, F32), rows_of(2 * len(kinds), F32)),
        in_specs=[HBM] * 5,
        out_specs=[VMEM] * 9,
        scratch_shapes=[pltpu.SMEM((docs,), jnp.int32), pltpu.SemaphoreType.DMA((5,))],
        compiler_params=params,
        cost_estimate=pl.CostEstimate(flops=2 * rows * width * width, bytes_accessed=4 * rows * width * 2, transcendentals=0),
        name="traded_state",
    )(*held)
    mate = send(other, mate_pairs(count))
    own, even, odd = pl.pallas_call(
        functools.partial(keep_kernel, reach),
        out_shape=(state,) * 3,
        in_specs=[VMEM] * 4,
        out_specs=[VMEM] * 3,
        compiler_params=params,
        cost_estimate=pl.CostEstimate(flops=2 * rows * width * width, bytes_accessed=2 * rows * width * 2, transcendentals=0),
        name="kept_state",
    )(own_left, own_right, weight, other)
    far = [
        (reach, "upper", send(even, group_pairs(count, reach, 0))),
        (reach, "lower", send(odd, group_pairs(count, reach, 1))),
    ]
    joined = own + flags[0] * mate
    joined = lax.optimization_barrier(joined)
    ringed = jnp.where(flags[2] > 0.5, far[0][2], joined)
    high_far, _ = lax.optimization_barrier((far[1][2], ringed))
    relayed = jnp.where(flags[1] > 0.5, far[0][2], high_far)
    near = [
        (reach - 1, "relay", send(relayed, mate_pairs(count)[2:-2])),
        (2, "ring", send(ringed, ring_pairs(count, 2, True))),
        *[(steps, "odd", send(joined, ring_pairs(count, steps, True))) for steps in range(4, reach - 1, 2)],
        *[(steps, "even", send(joined, swap_pairs(count, steps))) for steps in range(1, reach - 1, 2)],
    ]
    slots = [(1, "odd", mate)] + far + near
    received = [value for _, _, value in slots]
    assert kinds == [(steps, kind) for steps, kind, _ in slots]
    tensors = pl.pallas_call(
        inner_kernel,
        out_shape=(flat,) * 4 + (partial,) * 4,
        in_specs=[VMEM] * 5,
        out_specs=[VMEM] * 8,
        compiler_params=params,
        cost_estimate=pl.CostEstimate(flops=6 * 2 * rows * rows * width, bytes_accessed=4 * rows * width * 6, transcendentals=0),
        name="within_block",
    )(left, right, own_left, own_right, begin)
    return pl.pallas_call(
        outer_kernel,
        out_shape=(flat,) * 4,
        in_specs=[VMEM] * (10 + len(slots)),
        out_specs=[HBM] * 4,
        scratch_shapes=[pltpu.VMEM((rows, width), BF16)] * 4 + [pltpu.SemaphoreType.DMA((4,))],
        compiler_params=params,
        cost_estimate=pl.CostEstimate(flops=4 * 2 * rows * width * HD, bytes_accessed=4 * rows * width * 8, transcendentals=0),
        name="across_blocks",
    )(gates, begin, *tensors, *received)


def solution(mesh):
    in_specs = (P("ctx", "head"), P("ctx", "head"), P("ctx", "head"), P("ctx", "head"), P("head"))
    out_specs = (P("ctx", "head"), P("ctx", "head"), P("ctx", "head"), P("ctx", "head"))
    return jax.shard_map(body, mesh=mesh, in_specs=in_specs, out_specs=out_specs, check_vma=False)
```

```python
import functools

import jax
import jax.numpy as jnp
from jax import lax
from jax.experimental import pallas as pl
from jax.experimental.pallas import tpu as pltpu
from jax.sharding import PartitionSpec as P

HD = 128
F32 = jnp.float32
BF16 = jnp.bfloat16
HBM = pl.BlockSpec(memory_space=pltpu.HBM)
VMEM = pl.BlockSpec(memory_space=pltpu.VMEM)


def ring_pairs(count, steps, odd_up):
    out = []
    for j in range(count):
        target = j + steps if (j % 2 == 1) == odd_up else j - steps
        if not 0 <= target < count:
            target = j ^ 1
        out.append((j, target))
    return out


def swap_pairs(count, steps):
    pairs = [(j, j + steps) for j in range(1, count - steps, 2)]
    return pairs + [(b, a) for a, b in pairs]


def group_pairs(count, steps, first):
    pairs = [(j, j + steps) for j in range(count - steps) if j // steps % 2 == first]
    return pairs + [(b, a) for a, b in pairs]


def mate_pairs(count):
    return [(j, j ^ 1) for j in range(count)]


def send(value, pairs):
    blocks, groups = lax.axis_size("ctx"), lax.axis_size("head")
    spare = 1 if groups % 2 == 0 else 0
    rest = sorted(set(range(blocks)) - {a for a, _ in pairs})
    wide = [(a * groups + g, b * groups + g) for a, b in pairs for g in range(groups)]
    wide += [(a * groups + g, a * groups + (g ^ spare)) for a in rest for g in range(groups)]
    return lax.ppermute(value, ("ctx", "head"), wide)


def doc_edges(lengths_ref, base, rows):
    first_start = last_start = jnp.int32(0)
    first_finish = last_finish = jnp.int32(2**30)
    start = jnp.int32(0)
    starts = []
    for doc in range(lengths_ref.shape[0]):
        finish = start + lengths_ref[doc]
        starts.append(start)
        first_start = jnp.where(start <= base, start, first_start)
        last_start = jnp.where(start < base + rows, start, last_start)
        first_finish = jnp.where(finish > base, jnp.minimum(finish, first_finish), first_finish)
        last_finish = jnp.where(finish >= base + rows, jnp.minimum(finish, last_finish), last_finish)
        start = finish
    return starts, first_start, last_start, first_finish, last_finish


def row_begins(starts, base, rows):
    local = lax.broadcasted_iota(jnp.int32, (rows, HD), 0)
    begin = jnp.full((rows, HD), -base, jnp.int32)
    for start in starts:
        begin = jnp.where(local >= start - base, start - base, begin)
    return begin


def row_scales(begin):
    local = lax.broadcasted_iota(jnp.int32, begin.shape, 0)
    return lax.rsqrt((local - begin).astype(F32) + 1.0) * HD ** (-0.5)


def dot(a, b, contract):
    return lax.dot_general(a, b, (contract, ((), ())), preferred_element_type=F32)


def scaled_rows(rows, weights):
    return (rows.astype(F32) * jnp.concatenate([weights] * (rows.shape[1] // HD), axis=1)).astype(BF16)


def store_product(out_ref, left, right):
    for h in range(out_ref.shape[0]):
        part = slice(h * HD, (h + 1) * HD)
        out_ref[h] = dot(left[:, part], right[:, part], ((0,), (0,)))


def gate_of(place, rows, ends, steps, forward):
    _, first_start, _, _, last_finish = ends
    before = forward & (first_start < (place - steps + 1) * rows)
    after = jnp.logical_not(forward) & (last_finish > (place + steps) * rows)
    return before, after


def store_flags(out_ref, flags):
    for at, flag in enumerate(flags):
        out_ref[at : at + 1, :] = jnp.full((1, HD), jnp.where(flag, 1.0, 0.0), F32)


def trade_kernel(
    slots, reach, lengths_hbm, q_hbm, k_hbm, v_hbm, g_hbm,
    other_ref, left_ref, right_ref, own_left_ref, own_right_ref, weight_ref, begin_ref, flags_ref, gates_ref,
    lengths_ref, sems,
):
    rows = left_ref.shape[0]
    place = lax.axis_index("ctx")
    odd = place % 2 == 1
    lengths_copy = pltpu.make_async_copy(lengths_hbm, lengths_ref, sems.at[0])
    lengths_copy.start()
    targets = (left_ref, right_ref, own_left_ref, own_right_ref)

    def fetch(*sources):
        return [pltpu.make_async_copy(a, b, sems.at[1 + at]) for at, (a, b) in enumerate(zip(sources, targets))]

    @pl.when(odd)
    def _():
        for copy in fetch(q_hbm, g_hbm, k_hbm, v_hbm):
            copy.start()

    @pl.when(jnp.logical_not(odd))
    def _():
        for copy in fetch(k_hbm, v_hbm, q_hbm, g_hbm):
            copy.start()

    copies = fetch(q_hbm, g_hbm, k_hbm, v_hbm)
    base = place * rows
    lengths_copy.wait()
    ends = doc_edges(lengths_ref, base, rows)
    starts, first_start, last_start, first_finish, last_finish = ends
    begin = row_begins(starts, base, rows)
    begin_ref[...] = begin
    scales = row_scales(begin)
    local = lax.broadcasted_iota(jnp.int32, begin.shape, 0)
    tail = jnp.where(local >= last_start - base, 1.0, 0.0)
    head = jnp.where(local < first_finish - base, scales, 0.0)
    weight_ref[...] = jnp.where(odd, tail, head)
    weights = jnp.where(odd, head, tail)
    even = jnp.logical_not(odd)
    upper = place // reach % 2 == 1
    lower = jnp.logical_not(upper)
    count = lax.axis_size("ctx")
    keep = jnp.where(odd, last_start < base, first_finish > base + rows)
    store_flags(flags_ref, [keep, odd == upper, (place == 0) | (place == count - 1)])
    kinds = {"odd": odd, "ring": odd, "even": even, "relay": even, "upper": upper, "lower": lower}
    by_end = (place == 1) | (place == count - 2)
    gates = []
    for steps, kind in slots:
        before, after = gate_of(place, rows, ends, steps, kinds[kind])
        if kind == "relay":
            before, after = before & jnp.logical_not(by_end), after & jnp.logical_not(by_end)
        if kind == "ring":
            far_before, far_after = gate_of(place, rows, ends, reach - 1, even)
            before, after = before | (by_end & far_before), after | (by_end & far_after)
        gates += [before, after]
    store_flags(gates_ref, gates)
    copies[0].wait()
    left = scaled_rows(left_ref[...], weights)
    copies[1].wait()
    store_product(other_ref, left, right_ref[...])
    copies[2].wait()
    copies[3].wait()


def keep_kernel(reach, left_ref, right_ref, weight_ref, other_ref, own_ref, even_ref, odd_ref):
    place = lax.axis_index("ctx")
    crossed = (place % 2 == 1) == (place // reach % 2 == 1)
    store_product(own_ref, scaled_rows(left_ref[...], weight_ref[...]), right_ref[...])
    own, other = own_ref[...], other_ref[...]
    even_ref[...] = jnp.where(crossed, other, own)
    odd_ref[...] = jnp.where(crossed, own, other)


def inner_kernel(
    left_ref, right_ref, own_left_ref, own_right_ref, begin_ref,
    scaled_ref, k_ref, v_ref, g_ref, att_ref, gq_ref, gk_ref, gv_ref,
):
    rows, width = scaled_ref.shape
    odd = lax.axis_index("ctx") % 2 == 1
    left, right, own_left, own_right = left_ref[...], right_ref[...], own_left_ref[...], own_right_ref[...]
    scaled_ref[...] = scaled_rows(jnp.where(odd, left, own_left), row_scales(begin_ref[...]))
    k_ref[...] = jnp.where(odd, own_left, left)
    v_ref[...] = jnp.where(odd, own_right, right)
    g_ref[...] = jnp.where(odd, right, own_right)
    tile = min(256, rows)
    for at in range(0, rows, tile):
        reach = at + tile
        row_at = lax.broadcasted_iota(jnp.int32, (tile, reach), 0) + at
        column_at = lax.broadcasted_iota(jnp.int32, (tile, reach), 1)
        begin = jnp.concatenate([begin_ref[at:reach, :]] * (reach // HD), axis=1)
        allowed = (column_at <= row_at) & (column_at >= begin)
        for h in range(width // HD):
            part = slice(h * HD, (h + 1) * HD)
            scaled_t = scaled_ref[at:reach, part]
            grad_t = g_ref[at:reach, part]
            keys = k_ref[:reach, part]
            values = v_ref[:reach, part]
            scores = dot(scaled_t, keys, ((1,), (1,)))
            weights = jnp.where(allowed, scores, 0.0).astype(BF16)
            dscores = dot(grad_t, values, ((1,), (1,)))
            dweights = jnp.where(allowed, dscores, 0.0).astype(BF16)
            att_ref[at:reach, part] = dot(weights, values, ((1,), (0,)))
            gq_ref[at:reach, part] = dot(dweights, keys, ((1,), (0,)))
            grad_k = dot(dweights, scaled_t, ((0,), (0,)))
            grad_v = dot(weights, grad_t, ((0,), (0,)))
            if at:
                gk_ref[:at, part] += grad_k[:at]
                gv_ref[:at, part] += grad_v[:at]
            gk_ref[at:reach, part] = grad_k[at:]
            gv_ref[at:reach, part] = grad_v[at:]


def diagonal(blocks):
    zero = jnp.zeros((HD, HD), BF16)
    rows = [
        jnp.concatenate([block.astype(BF16) if h == at else zero for h in range(len(blocks))], axis=1)
        for at, block in enumerate(blocks)
    ]
    return jnp.concatenate(rows, axis=0)


def split(blocks):
    low = [block - block.astype(BF16).astype(F32) for block in blocks]
    return diagonal(blocks), diagonal(low)


def rounded(blocks):
    return (diagonal(blocks),)


def split_dot(rows, states, contract):
    total = dot(rows, states[0], contract)
    for state in states[1:]:
        total = total + dot(rows, state, contract)
    return total


def gated_states(gates_ref, slot_refs, first):
    heads = slot_refs[0].shape[0]
    entering = [jnp.zeros((HD, HD), F32)] * heads
    returning = [jnp.zeros((HD, HD), F32)] * heads
    for at, slot_ref in enumerate(slot_refs, first):
        before, after = gates_ref[2 * at : 2 * at + 1, :], gates_ref[2 * at + 1 : 2 * at + 2, :]
        entering = [state + before * slot_ref[h] for h, state in enumerate(entering)]
        returning = [state + after * slot_ref[h] for h, state in enumerate(returning)]
    return entering, returning


def outer_kernel(gates_ref, begin_ref, scaled_ref, k_ref, v_ref, g_ref, *refs):
    out_hbms, out_refs, sems = refs[-9:-5], refs[-5:-1], refs[-1]
    inner_refs, slot_refs = refs[:4], refs[4:-9]
    heads = scaled_ref.shape[1] // HD
    entering, returning = gated_states(gates_ref, slot_refs, 0)
    entering, returning = rounded(entering), rounded(returning)
    copies = [pltpu.make_async_copy(out_refs[at], out_hbms[at], sems.at[at]) for at in range(4)]
    attended = inner_refs[0][...] + split_dot(scaled_ref[...], entering, ((1,), (0,)))
    out_refs[0][...] = attended.astype(BF16)
    copies[0].start()
    scales = jnp.concatenate([row_scales(begin_ref[...])] * heads, axis=1)
    grad_q = inner_refs[1][...] + split_dot(g_ref[...], entering, ((1,), (1,)))
    out_refs[1][...] = (scales * grad_q).astype(BF16)
    copies[1].start()
    grad_k = inner_refs[2][...] + split_dot(v_ref[...], returning, ((1,), (1,)))
    out_refs[2][...] = grad_k.astype(BF16)
    copies[2].start()
    grad_v = inner_refs[3][...] + split_dot(k_ref[...], returning, ((1,), (0,)))
    out_refs[3][...] = grad_v.astype(BF16)
    copies[3].start()
    for copy in copies:
        copy.wait()


def body(query_rows, key_rows, value_rows, out_grad, doc_lengths):
    rows, width = query_rows.shape
    heads = width // HD
    docs = doc_lengths.shape[0]
    count = lax.axis_size("ctx")
    reach = count // 4
    arguments = (doc_lengths, query_rows, key_rows, value_rows, out_grad)
    held = [pltpu.with_memory_space_constraint(x, pltpu.HBM) for x in arguments]
    params = pltpu.CompilerParams(vmem_limit_bytes=32 * 2**20)
    state = jax.ShapeDtypeStruct((heads, HD, HD), F32)
    flat = jax.ShapeDtypeStruct((rows, width), BF16)
    partial = jax.ShapeDtypeStruct((rows, width), F32)
    kinds = [(1, "odd"), (reach, "upper"), (reach, "lower")] + [(reach - 1, "relay")] + [(2, "ring")] + [(steps, "odd") for steps in range(4, reach - 1, 2)] + [(steps, "even") for steps in range(1, reach - 1, 2)]
    rows_of = lambda n, kind: jax.ShapeDtypeStruct((n, HD), kind)
    other, left, right, own_left, own_right, weight, begin, flags, gates = pl.pallas_call(
        functools.partial(trade_kernel, tuple(kinds), reach),
        out_shape=(state,) + (flat,) * 4 + (rows_of(rows, F32), rows_of(rows, jnp.int32), rows_of(3, F32), rows_of(2 * len(kinds), F32)),
        in_specs=[HBM] * 5,
        out_specs=[VMEM] * 9,
        scratch_shapes=[pltpu.SMEM((docs,), jnp.int32), pltpu.SemaphoreType.DMA((5,))],
        compiler_params=params,
        cost_estimate=pl.CostEstimate(flops=2 * rows * width * width, bytes_accessed=4 * rows * width * 2, transcendentals=0),
        name="traded_state",
    )(*held)
    mate = send(other, mate_pairs(count))
    own, even, odd = pl.pallas_call(
        functools.partial(keep_kernel, reach),
        out_shape=(state,) * 3,
        in_specs=[VMEM] * 4,
        out_specs=[VMEM] * 3,
        compiler_params=params,
        cost_estimate=pl.CostEstimate(flops=2 * rows * width * width, bytes_accessed=2 * rows * width * 2, transcendentals=0),
        name="kept_state",
    )(own_left, own_right, weight, other)
    far = [
        (reach, "upper", send(even, group_pairs(count, reach, 0))),
        (reach, "lower", send(odd, group_pairs(count, reach, 1))),
    ]
    joined = own + flags[0] * mate
    joined = lax.optimization_barrier(joined)
    ringed = jnp.where(flags[2] > 0.5, far[0][2], joined)
    high_far, _ = lax.optimization_barrier((far[1][2], ringed))
    relayed = jnp.where(flags[1] > 0.5, far[0][2], high_far)
    near = [
        (reach - 1, "relay", send(relayed, mate_pairs(count)[2:-2])),
        (2, "ring", send(ringed, ring_pairs(count, 2, True))),
        *[(steps, "odd", send(joined, ring_pairs(count, steps, True))) for steps in range(4, reach - 1, 2)],
        *[(steps, "even", send(joined, swap_pairs(count, steps))) for steps in range(1, reach - 1, 2)],
    ]
    slots = [(1, "odd", mate)] + far + near
    received = [value for _, _, value in slots]
    assert kinds == [(steps, kind) for steps, kind, _ in slots]
    tensors = pl.pallas_call(
        inner_kernel,
        out_shape=(flat,) * 4 + (partial,) * 4,
        in_specs=[VMEM] * 5,
        out_specs=[VMEM] * 8,
        compiler_params=params,
        cost_estimate=pl.CostEstimate(flops=6 * 2 * rows * rows * width, bytes_accessed=4 * rows * width * 6, transcendentals=0),
        name="within_block",
    )(left, right, own_left, own_right, begin)
    return pl.pallas_call(
        outer_kernel,
        out_shape=(flat,) * 4,
        in_specs=[VMEM] * (10 + len(slots)),
        out_specs=[HBM] * 4,
        scratch_shapes=[pltpu.VMEM((rows, width), BF16)] * 4 + [pltpu.SemaphoreType.DMA((4,))],
        compiler_params=params,
        cost_estimate=pl.CostEstimate(flops=4 * 2 * rows * width * HD, bytes_accessed=4 * rows * width * 8, transcendentals=0),
        name="across_blocks",
    )(gates, begin, *tensors, *received)


def solution(mesh):
    in_specs = (P("ctx", "head"), P("ctx", "head"), P("ctx", "head"), P("ctx", "head"), P("head"))
    out_specs = (P("ctx", "head"), P("ctx", "head"), P("ctx", "head"), P("ctx", "head"))
    return jax.shard_map(body, mesh=mesh, in_specs=in_specs, out_specs=out_specs, check_vma=False)
```

```python
import functools

import jax
import jax.numpy as jnp
from jax import lax
from jax.experimental import pallas as pl
from jax.experimental.pallas import tpu as pltpu
from jax.sharding import PartitionSpec as P

HD = 128
F32 = jnp.float32
BF16 = jnp.bfloat16
HBM = pl.BlockSpec(memory_space=pltpu.HBM)
VMEM = pl.BlockSpec(memory_space=pltpu.VMEM)


def ring_pairs(count, steps):
    out = []
    for j in range(count):
        target = j + steps if j % 2 else j - steps
        if not 0 <= target < count:
            target = j ^ 1
        out.append((j, target))
    return out


def swap_pairs(count, steps):
    pairs = [(j, j + steps) for j in range(1, count - steps, 2)]
    return pairs + [(b, a) for a, b in pairs]


def group_pairs(count, steps, first):
    pairs = [(j, j + steps) for j in range(count - steps) if j // steps % 2 == first]
    return pairs + [(b, a) for a, b in pairs]


def mate_pairs(count):
    return [(j, j ^ 1) for j in range(count)]


def send(value, pairs):
    blocks, groups = lax.axis_size("ctx"), lax.axis_size("head")
    spare = 1 if groups % 2 == 0 else 0
    rest = sorted(set(range(blocks)) - {a for a, _ in pairs})
    wide = [(a * groups + g, b * groups + g) for a, b in pairs for g in range(groups)]
    wide += [(a * groups + g, a * groups + (g ^ spare)) for a in rest for g in range(groups)]
    return lax.ppermute(value, ("ctx", "head"), wide)


def doc_edges(lengths_ref, base, rows):
    first_start = last_start = jnp.int32(0)
    first_finish = last_finish = jnp.int32(2**30)
    start = jnp.int32(0)
    starts = []
    for doc in range(lengths_ref.shape[0]):
        finish = start + lengths_ref[doc]
        starts.append(start)
        first_start = jnp.where(start <= base, start, first_start)
        last_start = jnp.where(start < base + rows, start, last_start)
        first_finish = jnp.where(finish > base, jnp.minimum(finish, first_finish), first_finish)
        last_finish = jnp.where(finish >= base + rows, jnp.minimum(finish, last_finish), last_finish)
        start = finish
    return starts, first_start, last_start, first_finish, last_finish


def row_begins(starts, base, rows):
    local = lax.broadcasted_iota(jnp.int32, (rows, HD), 0)
    begin = jnp.full((rows, HD), -base, jnp.int32)
    for start in starts:
        begin = jnp.where(local >= start - base, start - base, begin)
    return begin


def row_scales(begin):
    local = lax.broadcasted_iota(jnp.int32, begin.shape, 0)
    return lax.rsqrt((local - begin).astype(F32) + 1.0) * HD ** (-0.5)


def dot(a, b, contract):
    return lax.dot_general(a, b, (contract, ((), ())), preferred_element_type=F32)


def scaled_rows(rows, weights):
    return (rows.astype(F32) * jnp.concatenate([weights] * (rows.shape[1] // HD), axis=1)).astype(BF16)


def store_product(out_ref, left, right):
    for h in range(out_ref.shape[0]):
        part = slice(h * HD, (h + 1) * HD)
        out_ref[h] = dot(left[:, part], right[:, part], ((0,), (0,)))


def gate_of(place, rows, ends, steps, forward):
    _, first_start, _, _, last_finish = ends
    before = forward & (first_start < (place - steps + 1) * rows)
    after = jnp.logical_not(forward) & (last_finish > (place + steps) * rows)
    return before, after


def store_flags(out_ref, flags):
    for at, flag in enumerate(flags):
        out_ref[at : at + 1, :] = jnp.full((1, HD), jnp.where(flag, 1.0, 0.0), F32)


def trade_kernel(
    slots, reach, lengths_hbm, q_hbm, k_hbm, v_hbm, g_hbm,
    other_ref, left_ref, right_ref, own_left_ref, own_right_ref, weight_ref, begin_ref, flags_ref, gates_ref,
    lengths_ref, sems,
):
    rows = left_ref.shape[0]
    place = lax.axis_index("ctx")
    odd = place % 2 == 1
    lengths_copy = pltpu.make_async_copy(lengths_hbm, lengths_ref, sems.at[0])
    lengths_copy.start()
    targets = (left_ref, right_ref, own_left_ref, own_right_ref)

    def fetch(*sources):
        return [pltpu.make_async_copy(a, b, sems.at[1 + at]) for at, (a, b) in enumerate(zip(sources, targets))]

    @pl.when(odd)
    def _():
        for copy in fetch(q_hbm, g_hbm, k_hbm, v_hbm):
            copy.start()

    @pl.when(jnp.logical_not(odd))
    def _():
        for copy in fetch(k_hbm, v_hbm, q_hbm, g_hbm):
            copy.start()

    copies = fetch(q_hbm, g_hbm, k_hbm, v_hbm)
    base = place * rows
    lengths_copy.wait()
    ends = doc_edges(lengths_ref, base, rows)
    starts, first_start, last_start, first_finish, last_finish = ends
    begin = row_begins(starts, base, rows)
    begin_ref[...] = begin
    scales = row_scales(begin)
    local = lax.broadcasted_iota(jnp.int32, begin.shape, 0)
    tail = jnp.where(local >= last_start - base, 1.0, 0.0)
    head = jnp.where(local < first_finish - base, scales, 0.0)
    weight_ref[...] = jnp.where(odd, tail, head)
    weights = jnp.where(odd, head, tail)
    even = jnp.logical_not(odd)
    upper = place // reach % 2 == 1
    lower = jnp.logical_not(upper)
    count = lax.axis_size("ctx")
    keep = jnp.where(odd, last_start < base, first_finish > base + rows)
    store_flags(flags_ref, [keep, odd == upper, (place == 0) | (place == count - 1)])
    kinds = {"odd": odd, "ring": odd, "even": even, "relay": even, "upper": upper, "lower": lower}
    by_end = (place == 1) | (place == count - 2)
    gates = []
    for steps, kind in slots:
        before, after = gate_of(place, rows, ends, steps, kinds[kind])
        if kind == "relay":
            before, after = before & jnp.logical_not(by_end), after & jnp.logical_not(by_end)
        if kind == "ring":
            far_before, far_after = gate_of(place, rows, ends, reach - 1, even)
            before, after = before | (by_end & far_before), after | (by_end & far_after)
        gates += [before, after]
    store_flags(gates_ref, gates)
    copies[0].wait()
    left = scaled_rows(left_ref[...], weights)
    copies[1].wait()
    store_product(other_ref, left, right_ref[...])
    copies[2].wait()
    copies[3].wait()


def keep_kernel(reach, left_ref, right_ref, weight_ref, other_ref, own_ref, even_ref, odd_ref):
    place = lax.axis_index("ctx")
    crossed = (place % 2 == 1) == (place // reach % 2 == 1)
    store_product(own_ref, scaled_rows(left_ref[...], weight_ref[...]), right_ref[...])
    own, other = own_ref[...], other_ref[...]
    even_ref[...] = jnp.where(crossed, other, own)
    odd_ref[...] = jnp.where(crossed, own, other)


def inner_kernel(
    left_ref, right_ref, own_left_ref, own_right_ref, begin_ref,
    scaled_ref, k_ref, v_ref, g_ref, att_ref, gq_ref, gk_ref, gv_ref,
):
    rows, width = scaled_ref.shape
    odd = lax.axis_index("ctx") % 2 == 1
    left, right, own_left, own_right = left_ref[...], right_ref[...], own_left_ref[...], own_right_ref[...]
    scaled_ref[...] = scaled_rows(jnp.where(odd, left, own_left), row_scales(begin_ref[...]))
    k_ref[...] = jnp.where(odd, own_left, left)
    v_ref[...] = jnp.where(odd, own_right, right)
    g_ref[...] = jnp.where(odd, right, own_right)
    tile = min(256, rows)
    for at in range(0, rows, tile):
        reach = at + tile
        row_at = lax.broadcasted_iota(jnp.int32, (tile, reach), 0) + at
        column_at = lax.broadcasted_iota(jnp.int32, (tile, reach), 1)
        begin = jnp.concatenate([begin_ref[at:reach, :]] * (reach // HD), axis=1)
        allowed = (column_at <= row_at) & (column_at >= begin)
        for h in range(width // HD):
            part = slice(h * HD, (h + 1) * HD)
            scaled_t = scaled_ref[at:reach, part]
            grad_t = g_ref[at:reach, part]
            keys = k_ref[:reach, part]
            values = v_ref[:reach, part]
            scores = dot(scaled_t, keys, ((1,), (1,)))
            weights = jnp.where(allowed, scores, 0.0).astype(BF16)
            dscores = dot(grad_t, values, ((1,), (1,)))
            dweights = jnp.where(allowed, dscores, 0.0).astype(BF16)
            att_ref[at:reach, part] = dot(weights, values, ((1,), (0,)))
            gq_ref[at:reach, part] = dot(dweights, keys, ((1,), (0,)))
            grad_k = dot(dweights, scaled_t, ((0,), (0,)))
            grad_v = dot(weights, grad_t, ((0,), (0,)))
            if at:
                gk_ref[:at, part] += grad_k[:at]
                gv_ref[:at, part] += grad_v[:at]
            gk_ref[at:reach, part] = grad_k[at:]
            gv_ref[at:reach, part] = grad_v[at:]


def split(blocks):
    high = [block.astype(BF16) for block in blocks]
    return [(top, (block - top.astype(F32)).astype(BF16)) for block, top in zip(blocks, high)]


def split_dot(rows, state, contract):
    out = []
    for h, parts in enumerate(state):
        left = rows[:, h * HD : (h + 1) * HD]
        out.append(dot(jnp.concatenate([left, left], axis=1), jnp.concatenate(parts, axis=contract[1][0]), contract))
    return jnp.concatenate(out, axis=1)


def outer_kernel(gates_ref, begin_ref, scaled_ref, k_ref, v_ref, g_ref, *refs):
    out_hbms, out_refs, sems = refs[-9:-5], refs[-5:-1], refs[-1]
    inner_refs, slot_refs = refs[:4], refs[4:-9]
    heads = scaled_ref.shape[1] // HD
    entering = [jnp.zeros((HD, HD), F32)] * heads
    returning = [jnp.zeros((HD, HD), F32)] * heads
    for at, slot_ref in enumerate(slot_refs):
        before, after = gates_ref[2 * at : 2 * at + 1, :], gates_ref[2 * at + 1 : 2 * at + 2, :]
        entering = [state + before * slot_ref[h] for h, state in enumerate(entering)]
        returning = [state + after * slot_ref[h] for h, state in enumerate(returning)]
    entering, returning = split(entering), split(returning)
    copies = [pltpu.make_async_copy(out_refs[at], out_hbms[at], sems.at[at]) for at in range(4)]
    scales = jnp.concatenate([row_scales(begin_ref[...])] * heads, axis=1)
    attended = inner_refs[0][...] + split_dot(scaled_ref[...], entering, ((1,), (0,)))
    out_refs[0][...] = attended.astype(BF16)
    copies[0].start()
    grad_q = inner_refs[1][...] + split_dot(g_ref[...], entering, ((1,), (1,)))
    out_refs[1][...] = (scales * grad_q).astype(BF16)
    copies[1].start()
    grad_k = inner_refs[2][...] + split_dot(v_ref[...], returning, ((1,), (1,)))
    out_refs[2][...] = grad_k.astype(BF16)
    copies[2].start()
    grad_v = inner_refs[3][...] + split_dot(k_ref[...], returning, ((1,), (0,)))
    out_refs[3][...] = grad_v.astype(BF16)
    copies[3].start()
    for copy in copies:
        copy.wait()


def body(query_rows, key_rows, value_rows, out_grad, doc_lengths):
    rows, width = query_rows.shape
    heads = width // HD
    docs = doc_lengths.shape[0]
    count = lax.axis_size("ctx")
    reach = count // 4
    arguments = (doc_lengths, query_rows, key_rows, value_rows, out_grad)
    held = [pltpu.with_memory_space_constraint(x, pltpu.HBM) for x in arguments]
    params = pltpu.CompilerParams(vmem_limit_bytes=32 * 2**20)
    state = jax.ShapeDtypeStruct((heads, HD, HD), F32)
    flat = jax.ShapeDtypeStruct((rows, width), BF16)
    partial = jax.ShapeDtypeStruct((rows, width), F32)
    far_kinds = [(1, "odd"), (reach, "upper"), (reach, "lower")]
    near_kinds = [(reach - 1, "relay"), (2, "ring")]
    near_kinds += [(steps, "odd") for steps in range(4, reach - 1, 2)]
    near_kinds += [(steps, "even") for steps in range(1, reach - 1, 2)]
    kinds = tuple(far_kinds + near_kinds)
    row_flags = [jax.ShapeDtypeStruct((n, HD), F32) for n in (3, 2 * len(kinds))]
    row_values = [jax.ShapeDtypeStruct((rows, HD), kind) for kind in (F32, jnp.int32)]
    other, left, right, own_left, own_right, weight, begin, flags, gates = pl.pallas_call(
        functools.partial(trade_kernel, kinds, reach),
        out_shape=(state, *(flat,) * 4, *row_values, *row_flags),
        in_specs=[HBM] * 5,
        out_specs=[VMEM] * 9,
        scratch_shapes=[pltpu.SMEM((docs,), jnp.int32), pltpu.SemaphoreType.DMA((5,))],
        compiler_params=params,
        cost_estimate=pl.CostEstimate(flops=2 * rows * width * width, bytes_accessed=4 * rows * width * 2, transcendentals=0),
        name="traded_state",
    )(*held)
    mate = send(other, mate_pairs(count))
    own, even, odd = pl.pallas_call(
        functools.partial(keep_kernel, reach),
        out_shape=(state,) * 3,
        in_specs=[VMEM] * 4,
        out_specs=[VMEM] * 3,
        compiler_params=params,
        cost_estimate=pl.CostEstimate(flops=2 * rows * width * width, bytes_accessed=2 * rows * width * 2, transcendentals=0),
        name="kept_state",
    )(own_left, own_right, weight, other)
    upward = send(even, group_pairs(count, reach, 0))
    downward = send(odd, group_pairs(count, reach, 1))
    joined = lax.optimization_barrier(own + flags[0] * mate)
    ringed = jnp.where(flags[2] > 0.5, upward, joined)
    late, _ = lax.optimization_barrier((downward, ringed))
    relayed = jnp.where(flags[1] > 0.5, upward, late)
    received = [mate, upward, downward]
    for steps, kind in near_kinds:
        if kind == "relay":
            received.append(send(relayed, mate_pairs(count)[2:-2]))
        elif kind == "even":
            received.append(send(joined, swap_pairs(count, steps)))
        else:
            received.append(send(ringed if kind == "ring" else joined, ring_pairs(count, steps)))
    tensors = pl.pallas_call(
        inner_kernel,
        out_shape=(flat,) * 4 + (partial,) * 4,
        in_specs=[VMEM] * 5,
        out_specs=[VMEM] * 8,
        compiler_params=params,
        cost_estimate=pl.CostEstimate(flops=6 * 2 * rows * rows * width, bytes_accessed=4 * rows * width * 6, transcendentals=0),
        name="within_block",
    )(left, right, own_left, own_right, begin)
    return pl.pallas_call(
        outer_kernel,
        out_shape=(flat,) * 4,
        in_specs=[VMEM] * (10 + len(received)),
        out_specs=[HBM] * 4,
        scratch_shapes=[pltpu.VMEM((rows, width), BF16)] * 4 + [pltpu.SemaphoreType.DMA((4,))],
        compiler_params=params,
        cost_estimate=pl.CostEstimate(flops=4 * 2 * rows * width * HD, bytes_accessed=4 * rows * width * 8, transcendentals=0),
        name="across_blocks",
    )(gates, begin, *tensors, *received)


def solution(mesh):
    in_specs = (P("ctx", "head"), P("ctx", "head"), P("ctx", "head"), P("ctx", "head"), P("head"))
    out_specs = (P("ctx", "head"), P("ctx", "head"), P("ctx", "head"), P("ctx", "head"))
    return jax.shard_map(body, mesh=mesh, in_specs=in_specs, out_specs=out_specs, check_vma=False)
```
